512 devices in a mesh: row: 32 (over x, z), col: 16 (over y, core).
Axes of the slice: x: 4, y: 8, z: 8, core: 2. Of those that a mesh axis runs over, the one named last changes fastest.
Arguments:
- load: float32 [3, 557568], P(None, ('row', 'col')), may hold values from -6 to 6
- node_mass: float32 [557568], P(('row', 'col')), may hold values from 0.05 to 0.5
- side_lists: int32 [2, 16896], P(None, ('row', 'col')), may hold values from 0 to 1088, as said below
- end_lists: int32 [2, 16896], P(None, ('row', 'col')), may hold values from 0 to 1088, as said below
- connect: int32 [3, 1048576], P(None, ('row', 'col')), may hold values from 0 to 1088, as said below
- geometry: float32 [4, 1048576], P(None, ('row', 'col')), may hold values from -4 to 4
- cover: float32 [1048576], P(('row', 'col')), may hold values from 0.1 to 2
- grazing: float32 [1048576], P(('row', 'col')), may hold values from 0 to 1
- rates: float32 [3], replicated, may hold values from 0.5 to 3
- elem_count: int32 [512], P(('row', 'col')), may hold values from 682 to 2048, as said below
- basis: float32 [32, 557568], P(None, ('row', 'col')), may hold values from -0.1875 to 0.1875
- coarse_inverse: bfloat16 [16384, 16384], P(('row', 'col')), as said below
Outputs:
- solution: float32 [3, 557568], P(None, ('row', 'col'))
- residual: float32 [3, 557568], P(None, ('row', 'col'))
- precond: float32 [3, 557568], P(None, ('row', 'col'))
The draws below stay inside these ranges and needn't reach their ends.
Inputs may be any that keep to these rules, and one draw needn't show every extreme that they name: connect holds local node numbers; each subdomain is a triangulated grid of 33 x 33 nodes with its nodes and elements numbered in a scattered order. side_lists[0] and side_lists[1] of a subdomain list its two edges toward the previous and next subdomain along col, each in an order that matches the neighbour's opposite list entry by entry; end_lists likewise along row; a corner node stands in one side list and one end list. `side_lists`: see connect. `end_lists`: see connect. A subdomain's live elements are its first elem_count slots; at least one subdomain is full and one holds the fewest. `coarse_inverse`: symmetric positive definite.
All inputs are finite; a program needn't handle non-finite values.
Results may differ from the reference program's by a relative error of at most 0.0003.
Values sent between devices are 32-bit elements; how exact they have to be, the bound alone decides.
A program may use at most 64 MiB of HBM per device.

```python
import math
import jax
import jax.numpy as jnp
from jax import lax

SIDE = 33
NL = 1089
EL_DEV = 2048
NC = 32
SAMPLES = 3
ITERS = 2
NCOARSE = 16384
NODES_TOT = 557568
EL_TOT = 1048576
N_ROW = 32
N_COL = 16


def mesh_tables(key):
    cells = (SIDE - 1) * (SIDE - 1)

    def one_device(index):
        device_key = jax.random.fold_in(key, index)
        node_perm = jax.random.permutation(jax.random.fold_in(device_key, 1), NL).astype(jnp.int32)
        cell_perm = jax.random.permutation(jax.random.fold_in(device_key, 2), cells).astype(jnp.int32)
        cell_x = cell_perm % (SIDE - 1)
        cell_y = cell_perm // (SIDE - 1)
        corner_a = cell_y * SIDE + cell_x
        corner_b = corner_a + 1
        corner_c = corner_a + SIDE
        corner_d = corner_c + 1
        first = jnp.stack([corner_a, corner_b, corner_d])
        second = jnp.stack([corner_a, corner_d, corner_c])
        grid = jnp.stack([first, second], axis=2).reshape(3, 2 * cells)
        conn_one = node_perm[grid]
        edge = jnp.arange(SIDE, dtype=jnp.int32)
        sides_one = jnp.stack([node_perm[edge * SIDE], node_perm[edge * SIDE + SIDE - 1]])
        ends_one = jnp.stack([node_perm[edge], node_perm[(SIDE - 1) * SIDE + edge]])
        return (conn_one, sides_one, ends_one)
    conn_all, sides_all, ends_all = jax.vmap(one_device)(jnp.arange(N_ROW * N_COL, dtype=jnp.int32))
    conn_all = jnp.transpose(conn_all, (1, 0, 2)).reshape(3, -1)
    sides_all = jnp.transpose(sides_all, (1, 0, 2)).reshape(2, -1)
    ends_all = jnp.transpose(ends_all, (1, 0, 2)).reshape(2, -1)
    return (conn_all.astype(jnp.int32), sides_all.astype(jnp.int32), ends_all.astype(jnp.int32))


def draw_connect(key, part):
    return mesh_tables(key)[0]


def draw_side_lists(key, part):
    return mesh_tables(key)[1]


def draw_end_lists(key, part):
    return mesh_tables(key)[2]


def draw_elem_count(key, part):
    key = jax.random.fold_in(key, 7)
    devices = N_ROW * N_COL
    fewest = EL_DEV // 3
    counts = jax.random.randint(jax.random.fold_in(key, 1), (devices,), fewest, EL_DEV + 1)
    full = jax.random.randint(jax.random.fold_in(key, 2), (), 0, devices)
    light = (full + 1 + jax.random.randint(jax.random.fold_in(key, 3), (), 0, devices - 1)) % devices
    places = jnp.arange(devices, dtype=jnp.int32)
    counts = jnp.where(places == light, fewest, counts)
    counts = jnp.where(places == full, EL_DEV, counts)
    return counts.astype(jnp.int32)


def draw_coarse_inverse(key, part):
    key = jax.random.fold_in(key, 11)
    spread = 0.25 / math.sqrt(NCOARSE)
    limit = spread * math.sqrt(3.0)
    noise = jax.random.uniform(jax.random.fold_in(key, 1), (NCOARSE, NCOARSE), jnp.float32, -limit, limit)
    upper = jnp.triu(noise, 1)
    diag_values = jnp.exp(jax.random.uniform(jax.random.fold_in(key, 2), (NCOARSE,), jnp.float32, math.log(0.75), math.log(1.5)))
    whole = upper + upper.T + jnp.diag(diag_values)
    return whole.astype(jnp.bfloat16)


def level_of(stream_key, extent, pieces, least, top_value):
    loudness, own = 1.0, jax.random.fold_in(stream_key, 6)
    for axis_at, shards_of in pieces:
        draws = jnp.exp(jax.random.uniform(jax.random.fold_in(own, axis_at), (shards_of,), jnp.float32, least / len(pieces), top_value / len(pieces)))
        loudness = loudness * jnp.repeat(draws, extent[axis_at] // shards_of).reshape([-1 if axis == axis_at else 1 for axis in range(len(extent))])
    return loudness


def normal_values(key, extent, deviation, most, shards=(), held_as=jnp.bfloat16):
    gain = level_of(key, extent, shards, -0.22, 0.18) if shards else 1.0
    entries = jax.random.normal(key, extent, jnp.float32) * deviation * gain
    return jnp.minimum(jnp.maximum(entries, -most), most).astype(held_as)


def setup_inputs(seed: int = 0) -> dict:
    streams_of = jax.random.split(jax.random.key(seed), 13)
    load = normal_values(streams_of[0], (SAMPLES, NODES_TOT), 1.0, 6.0, ((1, 512),), jnp.float32)
    node_mass = jnp.clip(jnp.exp(math.log(0.5) - 2.3025851 * jax.random.uniform(streams_of[1], (NODES_TOT,), jnp.float32) ** level_of(streams_of[1], (NODES_TOT,), ((0, 512),), -0.2, 0.2)), 0.05, 0.5)
    side_lists = draw_side_lists(jax.random.fold_in(streams_of[12], 71), 0)
    end_lists = draw_end_lists(jax.random.fold_in(streams_of[12], 71), 0)
    connect = draw_connect(jax.random.fold_in(streams_of[12], 71), 0)
    geometry = normal_values(streams_of[5], (4, EL_TOT), 1.0, 4.0, ((1, 512),), jnp.float32)
    cover = jnp.clip(jnp.exp(math.log(2.0) - 2.9957323 * jax.random.uniform(streams_of[6], (EL_TOT,), jnp.float32) ** level_of(streams_of[6], (EL_TOT,), ((0, 512),), -0.2, 0.2)), 0.1, 2.0)
    grazing = jnp.clip(1.0 * jax.random.uniform(streams_of[7], (EL_TOT,), jnp.float32) ** level_of(streams_of[7], (EL_TOT,), ((0, 512),), -0.2, 0.2), 0.0, 1.0)
    rates = jnp.clip(jax.random.uniform(streams_of[8], (SAMPLES,), jnp.float32, 0.5, 3.0), 0.5, 3.0)
    elem_count = draw_elem_count(jax.random.fold_in(streams_of[12], 71), 0)
    basis = normal_values(streams_of[10], (NC, NODES_TOT), NL ** -0.5, 0.1875, ((1, 512),), jnp.float32)
    coarse_inverse = draw_coarse_inverse(jax.random.fold_in(streams_of[12], 71), 0)
    return dict(load=load, node_mass=node_mass, side_lists=side_lists, end_lists=end_lists, connect=connect, geometry=geometry, cover=cover, grazing=grazing, rates=rates, elem_count=elem_count, basis=basis, coarse_inverse=coarse_inverse)


highest = lax.Precision.HIGHEST


def by_device(array):
    lead = array.shape[:-1]
    shaped = array.reshape(lead + (N_ROW, N_COL, array.shape[-1] // (N_ROW * N_COL)))
    return jnp.moveaxis(jnp.moveaxis(shaped, -3, 0), -2, 1)


def from_device(array):
    moved = jnp.moveaxis(jnp.moveaxis(array, 1, -2), 0, -3)
    return moved.reshape(moved.shape[:-3] + (-1,))


def over_devices(func):
    return jax.vmap(jax.vmap(func))


def pick_edges(vectors, edge_list):
    return jnp.stack([vectors[:, edge_list[0]], vectors[:, edge_list[1]]])


def add_edges(vectors, edge_list, from_low, from_high):
    vectors = vectors.at[:, edge_list[0]].add(from_low)
    return vectors.at[:, edge_list[1]].add(from_high)


def halo_sum(vectors, sides, ends):
    edges = over_devices(pick_edges)(vectors, sides)
    nothing = jnp.zeros_like(edges[:, :1, 1])
    from_low = jnp.concatenate([nothing, edges[:, :-1, 1]], axis=1)
    from_high = jnp.concatenate([edges[:, 1:, 0], nothing], axis=1)
    vectors = over_devices(add_edges)(vectors, sides, from_low, from_high)
    edges = over_devices(pick_edges)(vectors, ends)
    nothing = jnp.zeros_like(edges[:1, :, 1])
    from_low = jnp.concatenate([nothing, edges[:-1, :, 1]], axis=0)
    from_high = jnp.concatenate([edges[1:, :, 0], nothing], axis=0)
    return over_devices(add_edges)(vectors, ends, from_low, from_high)


def gradients(geometry):
    b_terms = jnp.stack([geometry[0], geometry[1], -geometry[0] - geometry[1]])
    c_terms = jnp.stack([geometry[2], geometry[3], -geometry[2] - geometry[3]])
    return b_terms, c_terms


def element_terms(vector, connect, geometry, conduct):
    b_terms, c_terms = gradients(geometry)
    corner = vector[:, connect]
    along_x = jnp.sum(b_terms[None] * corner, axis=1)
    along_y = jnp.sum(c_terms[None] * corner, axis=1)
    element_term = conduct[:, None, :] * (b_terms[None] * along_x[:, None, :] + c_terms[None] * along_y[:, None, :])
    return jnp.zeros_like(vector).at[:, connect.reshape(-1)].add(element_term.reshape(vector.shape[0], -1))


def diagonal_terms(mass, connect, geometry, conduct):
    b_terms, c_terms = gradients(geometry)
    element_term = conduct[:, None, :] * (b_terms * b_terms + c_terms * c_terms)[None]
    summed = jnp.zeros((conduct.shape[0], mass.shape[0]), jnp.float32)
    summed = summed.at[:, connect.reshape(-1)].add(element_term.reshape(conduct.shape[0], -1))
    return mass[None] + summed


def reference(load, node_mass, side_lists, end_lists, connect, geometry, cover, grazing, rates, elem_count, basis, coarse_inverse):
    load_dev = by_device(load)
    mass_dev = by_device(node_mass)
    sides = by_device(side_lists)
    ends = by_device(end_lists)
    conn_dev = by_device(connect)
    geom_dev = by_device(geometry)
    cover_dev = by_device(cover)
    graze_dev = by_device(grazing)
    count_dev = elem_count.reshape(N_ROW, N_COL)
    basis_dev = by_device(basis)

    def conductance(cover_one, graze_one, count_one):
        live_mask = (lax.iota(jnp.int32, cover_one.shape[0]) < count_one).astype(jnp.float32)
        return cover_one[None] * jnp.exp(-rates[:, None] * graze_one[None]) * live_mask[None]

    conduct = over_devices(conductance)(cover_dev, graze_dev, count_dev)
    diag_local = over_devices(diagonal_terms)(mass_dev, conn_dev, geom_dev, conduct)
    ones = jnp.ones_like(mass_dev)[:, :, None, :]
    stacked = halo_sum(jnp.concatenate([load_dev, diag_local, ones], axis=2), sides, ends)
    right_side = stacked[:, :, :SAMPLES]
    diagonal = stacked[:, :, SAMPLES:2 * SAMPLES]
    weight = 1.0 / stacked[:, :, 2 * SAMPLES]

    def operate(vectors):
        local_sum = over_devices(element_terms)(vectors, conn_dev, geom_dev, conduct) + mass_dev[:, :, None, :] * vectors
        return halo_sum(local_sum, sides, ends)

    def inner(first, second):
        return jnp.sum(weight[:, :, None, :] * first * second, axis=(0, 1, 3))

    blocks = coarse_inverse.reshape(N_ROW * N_COL, NC, NCOARSE)

    def precondition(residual):
        coarse_rhs = jnp.einsum("rcsn,rckn->rcsk", weight[:, :, None, :] * residual, basis_dev, precision=highest)
        coarse_all = jnp.moveaxis(coarse_rhs, 2, 0).reshape(SAMPLES, -1)
        coarse_sol = lax.map(lambda block: jnp.dot(coarse_all, block.astype(jnp.float32).T, precision=highest), blocks)
        coarse_sol = coarse_sol.reshape(N_ROW, N_COL, SAMPLES, NC)
        spread = jnp.einsum("rcsk,rckn->rcsn", coarse_sol, basis_dev, precision=highest) * weight[:, :, None, :]
        return residual / diagonal + halo_sum(spread, sides, ends)

    solution = jnp.zeros_like(right_side)
    residual = right_side
    precond = precondition(residual)
    fit_now = inner(residual, precond)
    direction = precond
    for sweep in range(ITERS):
        image = operate(direction)
        step_size = fit_now / inner(direction, image)
        solution = solution + step_size[:, None] * direction
        residual = residual - step_size[:, None] * image
        precond = precondition(residual)
        if sweep + 1 < ITERS:
            fit_next = inner(residual, precond)
            direction = precond + (fit_next / fit_now)[:, None] * direction
            fit_now = fit_next
    return from_device(solution), from_device(residual), from_device(precond)
```

```python
import functools

import jax
import jax.numpy as jnp
from jax import lax
from jax.experimental import pallas as pl
from jax.experimental.pallas import tpu as pltpu
from jax.sharding import PartitionSpec as P

MESH = pl.DeviceIdType.MESH
F32, BF16, I32 = jnp.float32, jnp.bfloat16, jnp.int32

NX, NZ, NY = 4, 8, 8
N_ROW, N_COL = 32, 16
SIDE, NL, EL, NC, SAMPLES = 33, 1089, 2048, 32, 3
NH = 9
GAP = 40
EMPTY = 36
AROUND = ((-1, -1), (-1, 1), (1, -1), (1, 1), (-1, 0), (1, 0), (0, -1), (0, 1))
HALOS = 7


def take(row, index):
    return jnp.take_along_axis(
        jnp.broadcast_to(row, index.shape), index, axis=1, mode="promise_in_bounds"
    )


def halves(value):
    high = value.astype(BF16)
    return high, (value - high.astype(F32)).astype(BF16)


def dot_lanes(left, right):
    return lax.dot_general(left, right, (((1,), (1,)), ((), ())), preferred_element_type=F32)


def dot_rows(left, right):
    return lax.dot_general(left, right, (((1,), (0,)), ((), ())), preferred_element_type=F32)


def over_groups(row):
    row = row + pltpu.roll(row, 64, 1)
    return row + pltpu.roll(row, 32, 1)


def kernel(
    load_ref, mass_ref, side_ref, end_ref, side_sm, end_sm, conn_ref, geom_ref, cover_ref, graze_ref,
    rates_sm, count_sm, basis_hbm, inv_hbm,
    sol_ref, res_ref, pre_ref,
    basis_ref, inv_ref, low_ref, high_ref, geo_ref, cond_ref, piece_ref, left_ref, hot_ref,
    mass_vm, slot_ref, list_ref, wide_ref, spread_ref, coarse_ref, all_ref, first_ref, node_ref,
    halo_out, halo_in,
    local_sem, hs_sem, hr_sem, ys_sem, yr_sem, zs_sem, zr_sem, xs_sem, xr_sem, cs_sem, cr_sem,
):
    row, col = lax.axis_index("row"), lax.axis_index("col")
    x, z, y, core = row // NZ, lax.rem(row, NZ), col // 2, lax.rem(col, 2)

    basis_copy = pltpu.make_async_copy(basis_hbm, basis_ref, local_sem.at[0])
    basis_copy.start()
    inv_copy = pltpu.make_async_copy(inv_hbm, inv_ref, local_sem.at[1])
    inv_copy.start()

    around = [(lax.rem(row + N_ROW + a, N_ROW), lax.rem(col + N_COL + b, N_COL)) for a, b in AROUND]
    along_y = [(row, lax.rem(y + k, NY) * 2 + core) for k in range(1, NY)]
    along_z = [(x * NZ + lax.rem(z + k, NZ), col) for k in range(1, NZ)]
    along_x = [(lax.rem(x + k, NX) * NZ + z, col) for k in range(1, NX)]
    other = [(row, y * 2 + 1 - core)]
    partners = around + along_y + along_z + along_x + other
    barrier = pltpu.get_barrier_semaphore()
    for device in partners:
        pl.semaphore_signal(barrier, inc=1, device_id=device, device_id_type=MESH)

    lanes8 = lax.broadcasted_iota(I32, (8, 128), 1)
    rows8 = lax.broadcasted_iota(I32, (8, 128), 0)
    rows16 = lax.broadcasted_iota(I32, (16, 128), 0)
    nodes = rows16 * 128 + lax.broadcasted_iota(I32, (16, 128), 1)
    lane_row = lax.broadcasted_iota(I32, (1, 128), 1)
    pending = []

    low_col, high_col = col > 0, col < N_COL - 1
    low_row, high_row = row > 0, row < N_ROW - 1
    slots = []
    for source, which in ((side_sm, 0), (side_sm, 1), (end_sm, 0), (end_sm, 1)):
        place = jnp.full((16, 128), EMPTY, I32)
        for pos in range(SIDE):
            place = jnp.where(nodes == source[which, pos], pos, place)
        slots.append(place)
    corner_slot = jnp.full((16, 128), EMPTY, I32)
    list_ref[...] = jnp.zeros((8, 128), I32)
    list_ref[0:2, 0:SIDE] = side_ref[...] + 1
    list_ref[2:4, 0:SIDE] = end_ref[...] + 1
    listed = list_ref[...]
    for i in range(2):
        for j in range(2):
            both = (slots[i] != EMPTY) & (slots[2 + j] != EMPTY)
            number = jnp.max(jnp.max(jnp.where(both, nodes, -1), axis=0, keepdims=True), axis=1, keepdims=True)
            listed = jnp.where((rows8 == 4) & (lanes8 == 2 * i + j), number + 1, listed)
            corner_slot = jnp.where(both, 2 * (1 - i) + (1 - j), corner_slot)
    slots.append(corner_slot)
    for k in range(5):
        slot_ref[k] = slots[k]
    listed = listed + pltpu.roll(listed, GAP, 1) + pltpu.roll(listed, 2 * GAP, 1) - 1
    sample_of = (lanes8 >= GAP).astype(I32) + (lanes8 >= 2 * GAP).astype(I32)
    edge_key = jnp.where(listed >= 0, sample_of * 16 + (listed >> 7), -1)
    edge_low = jnp.where(listed >= 0, listed & 127, 0)

    def one(flag):
        return jnp.where(flag, 1.0, 0.0).astype(F32)

    def shared(place, there):
        return jnp.where(place != EMPTY, one(there), 0.0)

    copies = (1.0 + shared(slots[0], low_col) + shared(slots[1], high_col)) * (
        1.0 + shared(slots[2], low_row) + shared(slots[3], high_row)
    )
    weight = 1.0 / copies

    def edge_tile(vectors):
        tile = jnp.zeros((8, 128), F32)
        for s in range(SAMPLES):
            for h in range(NH):
                tile = jnp.where(edge_key == s * 16 + h, take(vectors[s][h : h + 1, :], edge_low), tile)
        return tile

    def halo_start(slot, vectors):
        halo_out[slot] = edge_tile(vectors)
        copies = []
        for k, device in enumerate(around):
            copy = pltpu.make_async_remote_copy(
                src_ref=halo_out.at[slot], dst_ref=halo_in.at[slot, k],
                send_sem=hs_sem.at[slot, k], recv_sem=hr_sem.at[slot, k],
                device_id=device, device_id_type=MESH,
            )
            copy.start()
            copies.append(copy)
        pending.extend(copies)
        return copies

    def halo_finish(slot, copies, vectors):
        for copy in copies:
            copy.wait_recv()
        arrived = []
        for k, which, there in ((7, 1, low_col), (6, 0, high_col), (5, 3, low_row), (4, 2, high_row)):
            arrived.append(jnp.where(there, halo_in[slot, k, which : which + 1, :], 0.0))
        corner = jnp.zeros((1, 128), F32)
        in_list = lane_row - jnp.where(lane_row >= 2 * GAP, 2 * GAP, jnp.where(lane_row >= GAP, GAP, 0))
        for i in range(2):
            for j in range(2):
                k = AROUND.index((1 - 2 * j, 1 - 2 * i))
                there = (high_col if i else low_col) & (high_row if j else low_row)
                found = jnp.where(there, halo_in[slot, k, 4:5, :], 0.0)
                corner = jnp.where(in_list == 2 * (1 - i) + (1 - j), found, corner)
        arrived.append(corner)
        result = []
        for s in range(SAMPLES):
            total = vectors[s]
            for k in range(5):
                total = total + take(arrived[k], slot_ref[k] + GAP * s)
            result.append(total)
        return result

    node_ref[...] = jnp.zeros((SAMPLES, 16, 128), F32)
    mass_vm[...] = jnp.ones((16, 128), F32)
    for h in range(NH):
        width = min(128, NL - 128 * h)
        mass_vm[h : h + 1, 0:width] = mass_ref[0:1, 128 * h : 128 * h + width]
        for s in range(SAMPLES):
            node_ref[s, h : h + 1, 0:width] = load_ref[s : s + 1, 128 * h : 128 * h + width]
    load = [node_ref[s] for s in range(SAMPLES)]
    mass = mass_vm[...]
    pl.semaphore_wait(barrier, len(partners))
    load_halo = halo_start(0, load)

    for p in range(3):
        for j in range(16):
            number = conn_ref[p : p + 1, 128 * j : 128 * j + 128]
            low = number & 127
            low_ref[p, j : j + 1, :] = low
            high_ref[p, j : j + 1, :] = number >> 7
            hot = jnp.where(lax.broadcasted_iota(I32, (128, 128), 0) == low, 1.0, 0.0)
            hot_ref[:, p * EL + 128 * j : p * EL + 128 * j + 128] = hot.astype(BF16)
    for k in range(4):
        for j in range(16):
            geo_ref[k, j : j + 1, :] = geom_ref[k : k + 1, 128 * j : 128 * j + 128]
    live = nodes < count_sm[0]
    for s in range(SAMPLES):
        grown = cover_ref[...] * jnp.exp(-rates_sm[s] * graze_ref[...])
        cond_ref[s] = jnp.where(live, grown, 0.0)

    def gradients():
        g0, g1, g2, g3 = (geo_ref[k] for k in range(4))
        return (g0, g1, -g0 - g1), (g2, g3, -g2 - g3)

    def scatter(terms):
        for s in range(SAMPLES):
            for p in range(3):
                high = terms[s][p].astype(BF16).astype(F32)
                piece_ref[s, 0, p] = high
                piece_ref[s, 1, p] = terms[s][p] - high
        for p in range(3):
            for j in range(16):
                here = high_ref[p, j : j + 1, :] == rows16
                for s in range(SAMPLES):
                    for q in range(2):
                        value = jnp.where(here, piece_ref[s, q, p, j : j + 1, :], 0.0)
                        left_ref[32 * s + 16 * q : 32 * s + 16 * q + 16, p * EL + 128 * j : p * EL + 128 * j + 128] = (
                            value.astype(BF16)
                        )
        summed = dot_lanes(left_ref[...], hot_ref[...])
        return [summed[32 * s : 32 * s + 16] + summed[32 * s + 16 : 32 * s + 32] for s in range(SAMPLES)]

    def operate(vectors):
        b_terms, c_terms = gradients()
        terms = []
        for s in range(SAMPLES):
            corner = []
            for p in range(3):
                low, high = low_ref[p], high_ref[p]
                value = jnp.zeros((16, 128), F32)
                for h in range(NH):
                    value = jnp.where(high == h, take(vectors[s][h : h + 1, :], low), value)
                corner.append(value)
            along_b = b_terms[0] * corner[0] + b_terms[1] * corner[1] + b_terms[2] * corner[2]
            along_c = c_terms[0] * corner[0] + c_terms[1] * corner[1] + c_terms[2] * corner[2]
            along_b, along_c = cond_ref[s] * along_b, cond_ref[s] * along_c
            terms.append([b_terms[p] * along_b + c_terms[p] * along_c for p in range(3)])
        summed = scatter(terms)
        return [mass * vectors[s] + summed[s] for s in range(SAMPLES)]

    b_terms, c_terms = gradients()
    squares = [b_terms[p] * b_terms[p] + c_terms[p] * c_terms[p] for p in range(3)]
    diag = scatter([[cond_ref[s] * squares[p] for p in range(3)] for s in range(SAMPLES)])
    diag = [mass + diag[s] for s in range(SAMPLES)]
    diag_halo = halo_start(1, diag)

    basis_copy.wait()
    wide_ref[...] = jnp.zeros((12 * NC, 128), F32)
    for h in range(NH):
        width = min(128, NL - 128 * h)
        wide_ref[NC * h : NC * h + NC, 0:width] = (
            basis_ref[:, 128 * h : 128 * h + width] * weight[h : h + 1, 0:width]
        )
    wide_high, wide_low = halves(wide_ref[...])
    spread_ref[0 : 12 * NC] = wide_high
    spread_ref[12 * NC : 24 * NC] = wide_low

    own_group = lax.broadcasted_iota(I32, (16, 12 * NC), 0) == lax.broadcasted_iota(I32, (16, 12 * NC), 1) // NC

    def restrict(vectors):
        stacked = jnp.concatenate(vectors, axis=0)
        high, low = halves(stacked)
        both = dot_lanes(jnp.concatenate([high, low], axis=0), spread_ref[...])
        both = both[0:48, 0 : 12 * NC] + both[48:96, 0 : 12 * NC] + both[0:48, 12 * NC : 24 * NC]
        result = []
        for s in range(SAMPLES):
            kept = jnp.where(own_group, both[16 * s : 16 * s + 16], 0.0)
            kept = jnp.sum(kept, axis=0, keepdims=True)
            result.append(over_groups(kept[:, 0:128] + kept[:, 128:256] + kept[:, 256:384]))
        return result

    def prolong(coarse):
        pieces = []
        for s in range(SAMPLES):
            line = coarse[s]
            line = jnp.concatenate([line, line, line], axis=1)
            pieces.append(jnp.where(own_group, jnp.broadcast_to(line, (16, 12 * NC)), 0.0))
        high, low = halves(jnp.concatenate(pieces, axis=0))
        first = dot_rows(jnp.concatenate([high, low], axis=0), spread_ref[0 : 12 * NC])
        total = first[0:48] + first[48:96] + dot_rows(high, spread_ref[12 * NC : 24 * NC])
        return [total[16 * s : 16 * s + 16] for s in range(SAMPLES)]

    def coarse_setup():
        inv_copy.wait()
        into = lax.broadcasted_iota(I32, (256, 256), 1)
        from_lane = ((into & 127) >> 5) * 64 + (into >> 7) * 32 + (into & 31)
        move = jnp.where(lax.broadcasted_iota(I32, (256, 256), 0) == from_lane, 1.0, 0.0).astype(BF16)
        for m in range(64):
            part, t = m % 8, m // 8
            moved = dot_rows(inv_ref[:, 256 * m : 256 * m + 256], move).astype(BF16)
            for c in range(2):
                coarse_ref[c, NC * part : NC * part + NC, 128 * t : 128 * t + 128] = moved[:, 128 * c : 128 * c + 128]

    part_mask = lax.broadcasted_iota(I32, (32, 256), 0) // 4 == lax.broadcasted_iota(I32, (32, 256), 1) // NC

    def coarse_half(turn, which):
        pieces = []
        for t in range(8):
            pieces.append(all_ref[turn, pl.ds(pl.multiple_of(which * 256 + 32 * t, 32), 32), :])
        high, low = halves(jnp.concatenate(pieces, axis=1))
        both = dot_lanes(jnp.concatenate([high, low], axis=0), coarse_ref[which])
        return both[0:32] + both[32:64]

    def everyone(turn, rhs, scalars, between=None):
        sample = rows8 & 3
        tile = jnp.where(sample == 0, rhs[0], jnp.where(sample == 1, rhs[1], jnp.where(sample == 2, rhs[2], scalars)))
        mine = (rows8 >> 2 == y // 4) & (lanes8 >> 5 == lax.rem(y, 4))
        first_ref[turn, y] = jnp.where(mine, tile, 0.0)

        def send(refs, sends, recvs, devices):
            copies = []
            for k, device in enumerate(devices):
                copy = pltpu.make_async_remote_copy(
                    src_ref=refs, dst_ref=refs, send_sem=sends.at[turn, k], recv_sem=recvs.at[turn, k],
                    device_id=device, device_id_type=MESH,
                )
                copy.start()
                copies.append(copy)
            pending.extend(copies)
            return copies

        def arrive(copies):
            for copy in copies:
                copy.wait_recv()

        copies = send(first_ref.at[turn, y], ys_sem, yr_sem, along_y)
        if between is not None:
            between()
        arrive(copies)
        block = first_ref[turn, 0]
        for k in range(1, NY):
            block = block + first_ref[turn, k]
        base = pl.multiple_of((core * 32 + x * 8 + z) * 8, 8)
        all_ref[turn, pl.ds(base, 8), :] = block
        arrive(send(all_ref.at[turn, pl.ds(base, 8)], zs_sem, zr_sem, along_z))
        base = pl.multiple_of((core * 32 + x * 8) * 8, 64)
        arrive(send(all_ref.at[turn, pl.ds(base, 64)], xs_sem, xr_sem, along_x))
        base = pl.multiple_of(core * 256, 256)
        copies = send(all_ref.at[turn, pl.ds(base, 256)], cs_sem, cr_sem, other)
        total = coarse_half(turn, core)
        arrive(copies)
        total = jnp.where(part_mask, total + coarse_half(turn, 1 - core), 0.0)
        total = jnp.sum(total.reshape(4, 8, 256), axis=0)
        total = over_groups(total[:, 0:128] + total[:, 128:256])
        coarse = [total[s : s + 1] + total[s + 4 : s + 5] for s in range(SAMPLES)]
        if turn == 0:
            return coarse, None
        sums = all_ref[turn, 0:8, :]
        for k in range(1, 64):
            sums = sums + all_ref[turn, 8 * k : 8 * k + 8, :]
        return coarse, over_groups(sums[3:4] + sums[7:8])

    def scalar_line(rows):
        stacked = jnp.zeros((16, 128), F32)
        for k, value in enumerate(rows):
            stacked = jnp.where(rows16 == k, value, stacked)
        summed = jnp.sum(stacked, axis=1, keepdims=True)
        placed = jnp.where(rows16 == (lax.broadcasted_iota(I32, (16, 128), 1) & 31), summed, 0.0)
        return jnp.sum(placed, axis=0, keepdims=True)

    def over_nodes(value):
        return jnp.sum(value, axis=0, keepdims=True)

    def fit_row(residual, scale, rhs, coarse, s):
        own = over_nodes(weight * residual * residual * scale)
        return own + jnp.where(lane_row < NC, rhs[s] * coarse[s], 0.0)

    samples = range(SAMPLES)

    residual = halo_finish(0, load_halo, load)
    rhs = restrict(residual)
    coarse, _ = everyone(0, rhs, jnp.zeros((1, 128), F32), coarse_setup)
    diag = halo_finish(1, diag_halo, diag)
    inverse_diag = [1.0 / diag[s] for s in samples]
    spread = prolong(coarse)
    copies = halo_start(2, spread)
    spread = halo_finish(2, copies, spread)
    precond = [residual[s] * inverse_diag[s] + spread[s] for s in samples]

    direction = precond
    raw = operate(direction)
    copies = halo_start(3, raw)
    line = scalar_line(
        [fit_row(residual[s], inverse_diag[s], rhs, coarse, s) for s in samples]
        + [over_nodes(direction[s] * raw[s]) for s in samples]
    )
    image = halo_finish(3, copies, raw)
    image_rhs = restrict(image)
    image_coarse, sums = everyone(1, image_rhs, line)
    fit = [sums[:, s : s + 1] for s in samples]
    curved = [sums[:, 3 + s : 4 + s] for s in samples]
    step = [fit[s] / curved[s] for s in samples]
    coarse = [coarse[s] - step[s] * image_coarse[s] for s in samples]
    spread = prolong(coarse)
    copies = halo_start(4, spread)
    solution = [step[s] * direction[s] for s in samples]
    residual = [residual[s] - step[s] * image[s] for s in samples]
    rhs = [rhs[s] - step[s] * image_rhs[s] for s in samples]
    spread = halo_finish(4, copies, spread)
    precond = [residual[s] * inverse_diag[s] + spread[s] for s in samples]

    fresh = operate(precond)
    copies = halo_start(5, fresh)
    line = scalar_line(
        [fit_row(residual[s], inverse_diag[s], rhs, coarse, s) for s in samples]
        + [over_nodes(precond[s] * fresh[s]) for s in samples]
        + [over_nodes(precond[s] * raw[s]) for s in samples]
    )
    fresh_image = halo_finish(5, copies, fresh)
    fresh_rhs = restrict(fresh_image)
    fresh_coarse, sums = everyone(2, fresh_rhs, line)
    fit_next = [sums[:, s : s + 1] for s in samples]
    ratio = [fit_next[s] / fit[s] for s in samples]
    curved = [
        sums[:, 3 + s : 4 + s] + ratio[s] * (2.0 * sums[:, 6 + s : 7 + s] + ratio[s] * curved[s]) for s in samples
    ]
    step = [fit_next[s] / curved[s] for s in samples]
    coarse = [coarse[s] - step[s] * (fresh_coarse[s] + ratio[s] * image_coarse[s]) for s in samples]
    spread = prolong(coarse)
    copies = halo_start(6, spread)
    solution = [solution[s] + step[s] * (precond[s] + ratio[s] * direction[s]) for s in samples]
    residual = [residual[s] - step[s] * (fresh_image[s] + ratio[s] * image[s]) for s in samples]

    def put(ref, values):
        for s in samples:
            for h in range(NH):
                width = min(128, NL - 128 * h)
                ref[s : s + 1, 128 * h : 128 * h + width] = values[s][h : h + 1, 0:width]

    put(sol_ref, solution)
    put(res_ref, residual)
    spread = halo_finish(6, copies, spread)
    put(pre_ref, [residual[s] * inverse_diag[s] + spread[s] for s in samples])
    for copy in pending:
        copy.wait_send()


def body(
    load, node_mass, side_lists, end_lists, connect, geometry, cover, grazing, rates, elem_count, basis, coarse_inverse
):
    vmem = pl.BlockSpec(memory_space=pltpu.VMEM)
    smem = pl.BlockSpec(memory_space=pltpu.SMEM)
    hbm = pl.BlockSpec(memory_space=pl.ANY)
    dma = pltpu.SemaphoreType.DMA
    return pl.pallas_call(
        kernel,
        out_shape=[jax.ShapeDtypeStruct((SAMPLES, NL), F32)] * 3,
        in_specs=[vmem, vmem, vmem, vmem, smem, smem, vmem, vmem, vmem, vmem, smem, smem, hbm, hbm],
        out_specs=[vmem] * 3,
        scratch_shapes=[
            pltpu.VMEM((NC, NL), F32),
            pltpu.VMEM((NC, 512 * NC), BF16),
            pltpu.VMEM((3, 16, 128), I32),
            pltpu.VMEM((3, 16, 128), I32),
            pltpu.VMEM((4, 16, 128), F32),
            pltpu.VMEM((SAMPLES, 16, 128), F32),
            pltpu.VMEM((SAMPLES, 2, 3, 16, 128), F32),
            pltpu.VMEM((96, 3 * EL), BF16),
            pltpu.VMEM((128, 3 * EL), BF16),
            pltpu.VMEM((16, 128), F32),
            pltpu.VMEM((5, 16, 128), I32),
            pltpu.VMEM((8, 128), I32),
            pltpu.VMEM((12 * NC, 128), F32),
            pltpu.VMEM((24 * NC, 128), BF16),
            pltpu.VMEM((2, 256, 1024), BF16),
            pltpu.VMEM((3, 512, 128), F32),
            pltpu.VMEM((3, NY, 8, 128), F32),
            pltpu.VMEM((SAMPLES, 16, 128), F32),
            pltpu.VMEM((HALOS, 8, 128), F32),
            pltpu.VMEM((HALOS, 8, 8, 128), F32),
            dma((2,)),
            dma((HALOS, 8)), dma((HALOS, 8)),
            dma((3, NY - 1)), dma((3, NY - 1)),
            dma((3, NZ - 1)), dma((3, NZ - 1)),
            dma((3, NX - 1)), dma((3, NX - 1)),
            dma((3, 1)), dma((3, 1)),
        ],
        compiler_params=pltpu.CompilerParams(
            collective_id=0, has_side_effects=True, vmem_limit_bytes=40 * 2**20
        ),
    )(
        load, node_mass.reshape(1, NL), side_lists, end_lists, side_lists, end_lists, connect, geometry,
        cover.reshape(16, 128), grazing.reshape(16, 128), rates, elem_count, basis, coarse_inverse,
    )


def solution(mesh):
    both = ("row", "col")
    return jax.shard_map(
        body,
        mesh=mesh,
        in_specs=(
            P(None, both), P(both), P(None, both), P(None, both), P(None, both), P(None, both),
            P(both), P(both), P(), P(both), P(None, both), P(both, None),
        ),
        out_specs=(P(None, both), P(None, both), P(None, both)),
        check_vma=False,
    )
```

```python
import functools

import jax
import jax.numpy as jnp
from jax import lax
from jax.experimental import pallas as pl
from jax.experimental.pallas import tpu as pltpu
from jax.sharding import PartitionSpec as P

MESH = pl.DeviceIdType.MESH
F32, BF16, I32 = jnp.float32, jnp.bfloat16, jnp.int32

NX, NZ, NY = 4, 8, 8
N_ROW, N_COL = 32, 16
SIDE, NL, EL, NC, SAMPLES = 33, 1089, 2048, 32, 3
NH = 9
GAP = 40
EMPTY = 36
AROUND = ((-1, -1), (-1, 1), (1, -1), (1, 1), (-1, 0), (1, 0), (0, -1), (0, 1))
HALOS = 7


def take(row, index):
    return jnp.take_along_axis(
        jnp.broadcast_to(row, index.shape), index, axis=1, mode="promise_in_bounds"
    )


def halves(value):
    high = value.astype(BF16)
    return high, (value - high.astype(F32)).astype(BF16)


def dot_lanes(left, right):
    return lax.dot_general(left, right, (((1,), (1,)), ((), ())), preferred_element_type=F32)


def dot_rows(left, right):
    return lax.dot_general(left, right, (((1,), (0,)), ((), ())), preferred_element_type=F32)


def over_groups(row):
    row = row + pltpu.roll(row, 64, 1)
    return row + pltpu.roll(row, 32, 1)


def kernel(
    load_hbm, mass_hbm, side_hbm, end_hbm, conn_hbm, geom_hbm, cover_hbm, graze_hbm,
    rates_hbm, count_hbm, basis_hbm, inv_hbm,
    sol_ref, res_ref, pre_ref,
    load_ref, mass_ref, side_ref, end_ref, side_sm, end_sm, conn_ref, geom_ref, cover_ref, graze_ref,
    rates_sm, count_sm, basis_ref, inv_ref, low_ref, high_ref, geo_ref, cond_ref, piece_ref, left_ref, hot_ref,
    mass_vm, slot_ref, list_ref, wide_ref, spread_ref, coarse_ref, all_ref, first_ref, node_ref,
    halo_out, halo_in,
    local_sem, hs_sem, hr_sem, ps_sem, pr_sem, zs_sem, zr_sem, cs_sem, cr_sem,
):
    row, col = lax.axis_index("row"), lax.axis_index("col")
    x, z, y, core = row // NZ, lax.rem(row, NZ), col // 2, lax.rem(col, 2)

    loads = []
    for source, target in (
        (side_hbm, side_sm), (end_hbm, end_sm), (side_hbm, side_ref), (end_hbm, end_ref), (load_hbm, load_ref),
        (mass_hbm, mass_ref), (conn_hbm, conn_ref), (geom_hbm, geom_ref), (cover_hbm, cover_ref),
        (graze_hbm, graze_ref), (rates_hbm, rates_sm), (count_hbm, count_sm), (basis_hbm, basis_ref), (inv_hbm, inv_ref),
    ):
        loads.append(pltpu.make_async_copy(source, target, local_sem.at[len(loads)]))
        loads[-1].start()
    basis_copy, inv_copy = loads[12:]

    around = [(lax.rem(row + N_ROW + a, N_ROW), lax.rem(col + N_COL + b, N_COL)) for a, b in AROUND]
    offsets = sorted(
        ((a, b) for a in range(NX) for b in range(NY) if a or b), key=lambda o: -min(o[0], NX - o[0]) - min(o[1], NY - o[1])
    )
    plane = [(lax.rem(x + a, NX) * NZ + z, lax.rem(y + b, NY) * 2 + core) for a, b in offsets]
    along_z = [(x * NZ + lax.rem(z + k, NZ), col) for k in (4, 3, 5, 2, 6, 1, 7)]
    other = [(row, y * 2 + 1 - core)]
    partners = around + plane + along_z + other
    barrier = pltpu.get_barrier_semaphore()
    for device in partners:
        pl.semaphore_signal(barrier, inc=1, device_id=device, device_id_type=MESH)

    lanes8 = lax.broadcasted_iota(I32, (8, 128), 1)
    rows8 = lax.broadcasted_iota(I32, (8, 128), 0)
    rows16 = lax.broadcasted_iota(I32, (16, 128), 0)
    nodes = rows16 * 128 + lax.broadcasted_iota(I32, (16, 128), 1)
    lane_row = lax.broadcasted_iota(I32, (1, 128), 1)
    pending = []

    for copy in loads[:6]:
        copy.wait()
    low_col, high_col = col > 0, col < N_COL - 1
    low_row, high_row = row > 0, row < N_ROW - 1
    slots = []
    for source, which in ((side_sm, 0), (side_sm, 1), (end_sm, 0), (end_sm, 1)):
        place = jnp.full((16, 128), EMPTY, I32)
        for pos in range(SIDE):
            place = jnp.where(nodes == source[which, pos], pos, place)
        slots.append(place)
    corner_slot = jnp.full((16, 128), EMPTY, I32)
    list_ref[...] = jnp.zeros((8, 128), I32)
    list_ref[0:2, 0:SIDE] = side_ref[...] + 1
    list_ref[2:4, 0:SIDE] = end_ref[...] + 1
    listed = list_ref[...]
    for i in range(2):
        for j in range(2):
            both = (slots[i] != EMPTY) & (slots[2 + j] != EMPTY)
            number = jnp.max(jnp.max(jnp.where(both, nodes, -1), axis=0, keepdims=True), axis=1, keepdims=True)
            listed = jnp.where((rows8 == 4) & (lanes8 == 2 * i + j), number + 1, listed)
            corner_slot = jnp.where(both, 2 * (1 - i) + (1 - j), corner_slot)
    slots.append(corner_slot)
    for k in range(5):
        slot_ref[k] = slots[k]
    listed = listed + pltpu.roll(listed, GAP, 1) + pltpu.roll(listed, 2 * GAP, 1) - 1
    sample_of = (lanes8 >= GAP).astype(I32) + (lanes8 >= 2 * GAP).astype(I32)
    edge_key = jnp.where(listed >= 0, sample_of * 16 + (listed >> 7), -1)
    edge_low = jnp.where(listed >= 0, listed & 127, 0)

    def one(flag):
        return jnp.where(flag, 1.0, 0.0).astype(F32)

    def shared(place, there):
        return jnp.where(place != EMPTY, one(there), 0.0)

    copies = (1.0 + shared(slots[0], low_col) + shared(slots[1], high_col)) * (
        1.0 + shared(slots[2], low_row) + shared(slots[3], high_row)
    )
    weight = 1.0 / copies

    def edge_tile(vectors):
        tile = jnp.zeros((8, 128), F32)
        for s in range(SAMPLES):
            for h in range(NH):
                tile = jnp.where(edge_key == s * 16 + h, take(vectors[s][h : h + 1, :], edge_low), tile)
        return tile

    def halo_start(slot, vectors):
        halo_out[slot] = edge_tile(vectors)
        copies = []
        for k, device in enumerate(around):
            copy = pltpu.make_async_remote_copy(
                src_ref=halo_out.at[slot], dst_ref=halo_in.at[slot, k],
                send_sem=hs_sem.at[slot, k], recv_sem=hr_sem.at[slot, k],
                device_id=device, device_id_type=MESH,
            )
            copy.start()
            copies.append(copy)
        pending.extend(copies)
        return copies

    def halo_finish(slot, copies, vectors):
        for copy in copies:
            copy.wait_recv()
        arrived = []
        for k, which, there in ((7, 1, low_col), (6, 0, high_col), (5, 3, low_row), (4, 2, high_row)):
            arrived.append(jnp.where(there, halo_in[slot, k, which : which + 1, :], 0.0))
        corner = jnp.zeros((1, 128), F32)
        in_list = lane_row - jnp.where(lane_row >= 2 * GAP, 2 * GAP, jnp.where(lane_row >= GAP, GAP, 0))
        for i in range(2):
            for j in range(2):
                k = AROUND.index((1 - 2 * j, 1 - 2 * i))
                there = (high_col if i else low_col) & (high_row if j else low_row)
                found = jnp.where(there, halo_in[slot, k, 4:5, :], 0.0)
                corner = jnp.where(in_list == 2 * (1 - i) + (1 - j), found, corner)
        arrived.append(corner)
        result = []
        for s in range(SAMPLES):
            total = vectors[s]
            for k in range(5):
                total = total + take(arrived[k], slot_ref[k] + GAP * s)
            result.append(total)
        return result

    node_ref[...] = jnp.zeros((SAMPLES, 16, 128), F32)
    mass_vm[...] = jnp.ones((16, 128), F32)
    for h in range(NH):
        width = min(128, NL - 128 * h)
        mass_vm[h : h + 1, 0:width] = mass_ref[128 * h : 128 * h + width].reshape(1, width)
        for s in range(SAMPLES):
            node_ref[s, h : h + 1, 0:width] = load_ref[s : s + 1, 128 * h : 128 * h + width]
    load = [node_ref[s] for s in range(SAMPLES)]
    mass = mass_vm[...]
    pl.semaphore_wait(barrier, len(partners))
    load_halo = halo_start(0, load)

    for copy in loads[6:12]:
        copy.wait()
    for p in range(3):
        for j in range(16):
            number = conn_ref[p : p + 1, 128 * j : 128 * j + 128]
            low = number & 127
            low_ref[p, j : j + 1, :] = low
            high_ref[p, j : j + 1, :] = number >> 7
            hot = jnp.where(lax.broadcasted_iota(I32, (128, 128), 0) == low, 1.0, 0.0)
            hot_ref[:, p * EL + 128 * j : p * EL + 128 * j + 128] = hot.astype(BF16)
    for k in range(4):
        for j in range(16):
            geo_ref[k, j : j + 1, :] = geom_ref[k : k + 1, 128 * j : 128 * j + 128]
    live = nodes < count_sm[0]
    for s in range(SAMPLES):
        grown = cover_ref[...] * jnp.exp(-rates_sm[s] * graze_ref[...])
        cond_ref[s] = jnp.where(live, grown, 0.0)

    def gradients():
        g0, g1, g2, g3 = (geo_ref[k] for k in range(4))
        return (g0, g1, -g0 - g1), (g2, g3, -g2 - g3)

    def scatter(terms):
        for s in range(SAMPLES):
            for p in range(3):
                high = terms[s][p].astype(BF16).astype(F32)
                piece_ref[s, 0, p] = high
                piece_ref[s, 1, p] = terms[s][p] - high
        for p in range(3):
            for j in range(16):
                here = high_ref[p, j : j + 1, :] == rows16
                for s in range(SAMPLES):
                    for q in range(2):
                        value = jnp.where(here, piece_ref[s, q, p, j : j + 1, :], 0.0)
                        left_ref[32 * s + 16 * q : 32 * s + 16 * q + 16, p * EL + 128 * j : p * EL + 128 * j + 128] = (
                            value.astype(BF16)
                        )
        summed = dot_lanes(left_ref[...], hot_ref[...])
        return [summed[32 * s : 32 * s + 16] + summed[32 * s + 16 : 32 * s + 32] for s in range(SAMPLES)]

    def operate(vectors):
        b_terms, c_terms = gradients()
        terms = []
        for s in range(SAMPLES):
            corner = []
            for p in range(3):
                low, high = low_ref[p], high_ref[p]
                value = jnp.zeros((16, 128), F32)
                for h in range(NH):
                    value = jnp.where(high == h, take(vectors[s][h : h + 1, :], low), value)
                corner.append(value)
            along_b = b_terms[0] * corner[0] + b_terms[1] * corner[1] + b_terms[2] * corner[2]
            along_c = c_terms[0] * corner[0] + c_terms[1] * corner[1] + c_terms[2] * corner[2]
            along_b, along_c = cond_ref[s] * along_b, cond_ref[s] * along_c
            terms.append([b_terms[p] * along_b + c_terms[p] * along_c for p in range(3)])
        summed = scatter(terms)
        return [mass * vectors[s] + summed[s] for s in range(SAMPLES)]

    b_terms, c_terms = gradients()
    squares = [b_terms[p] * b_terms[p] + c_terms[p] * c_terms[p] for p in range(3)]
    diag = scatter([[cond_ref[s] * squares[p] for p in range(3)] for s in range(SAMPLES)])
    diag = [mass + diag[s] for s in range(SAMPLES)]
    diag_halo = halo_start(1, diag)

    basis_copy.wait()
    wide_ref[...] = jnp.zeros((12 * NC, 128), F32)
    for h in range(NH):
        width = min(128, NL - 128 * h)
        wide_ref[NC * h : NC * h + NC, 0:width] = (
            basis_ref[:, 128 * h : 128 * h + width] * weight[h : h + 1, 0:width]
        )
    wide_high, wide_low = halves(wide_ref[...])
    spread_ref[0 : 12 * NC] = wide_high
    spread_ref[12 * NC : 24 * NC] = wide_low

    own_group = lax.broadcasted_iota(I32, (16, 12 * NC), 0) == lax.broadcasted_iota(I32, (16, 12 * NC), 1) // NC

    def restrict(vectors):
        stacked = jnp.concatenate(vectors, axis=0)
        high, low = halves(stacked)
        both = dot_lanes(jnp.concatenate([high, low], axis=0), spread_ref[...])
        both = both[0:48, 0 : 12 * NC] + both[48:96, 0 : 12 * NC] + both[0:48, 12 * NC : 24 * NC]
        result = []
        for s in range(SAMPLES):
            kept = jnp.where(own_group, both[16 * s : 16 * s + 16], 0.0)
            kept = jnp.sum(kept, axis=0, keepdims=True)
            result.append(over_groups(kept[:, 0:128] + kept[:, 128:256] + kept[:, 256:384]))
        return result

    def prolong(coarse):
        pieces = []
        for s in range(SAMPLES):
            line = coarse[s]
            line = jnp.concatenate([line, line, line], axis=1)
            pieces.append(jnp.where(own_group, jnp.broadcast_to(line, (16, 12 * NC)), 0.0))
        high, low = halves(jnp.concatenate(pieces, axis=0))
        first = dot_rows(jnp.concatenate([high, low], axis=0), spread_ref[0 : 12 * NC])
        total = first[0:48] + first[48:96] + dot_rows(high, spread_ref[12 * NC : 24 * NC])
        return [total[16 * s : 16 * s + 16] for s in range(SAMPLES)]

    def coarse_setup():
        inv_copy.wait()
        into = lax.broadcasted_iota(I32, (256, 256), 1)
        from_lane = ((into & 127) >> 5) * 64 + (into >> 7) * 32 + (into & 31)
        move = jnp.where(lax.broadcasted_iota(I32, (256, 256), 0) == from_lane, 1.0, 0.0).astype(BF16)
        for m in range(64):
            part, t = m // 16 * 2 + m % 2, m // 2 % 8
            moved = dot_rows(inv_ref[:, 256 * m : 256 * m + 256], move).astype(BF16)
            for c in range(2):
                coarse_ref[c, NC * part : NC * part + NC, 128 * t : 128 * t + 128] = moved[:, 128 * c : 128 * c + 128]

    part_mask = lax.broadcasted_iota(I32, (32, 256), 0) // 4 == lax.broadcasted_iota(I32, (32, 256), 1) // NC

    def coarse_half(turn, which):
        pieces = []
        for t in range(8):
            pieces.append(all_ref[turn, pl.ds(pl.multiple_of(which * 256 + 32 * t, 32), 32), :])
        high, low = halves(jnp.concatenate(pieces, axis=1))
        both = dot_lanes(jnp.concatenate([high, low], axis=0), coarse_ref[which])
        return both[0:32] + both[32:64]

    def everyone(turn, rhs, scalars, between=None):
        rows4 = lax.broadcasted_iota(I32, (4, 128), 0)
        tile = jnp.where(rows4 == 0, rhs[0], jnp.where(rows4 == 1, rhs[1], jnp.where(rows4 == 2, rhs[2], scalars)))
        mine = lax.broadcasted_iota(I32, (4, 128), 1) >> 5 == lax.rem(y, 4)
        first_ref[turn, x * NY + y] = jnp.where(mine, tile, 0.0)

        def send(refs, sends, recvs, devices):
            copies = []
            for k, device in enumerate(devices):
                copy = pltpu.make_async_remote_copy(
                    src_ref=refs, dst_ref=refs, send_sem=sends.at[turn, k], recv_sem=recvs.at[turn, k],
                    device_id=device, device_id_type=MESH,
                )
                copy.start()
                copies.append(copy)
            pending.extend(copies)
            return copies

        def arrive(copies):
            for copy in copies:
                copy.wait_recv()

        copies = send(first_ref.at[turn, x * NY + y], ps_sem, pr_sem, plane)
        if between is not None:
            between()
        arrive(copies)
        base = (core * NZ + z) * 32
        for k in range(NX):
            fours = []
            for q in range(2):
                four = first_ref[turn, k * NY + 4 * q]
                for j in range(1, 4):
                    four = four + first_ref[turn, k * NY + 4 * q + j]
                fours.append(four)
            all_ref[turn, pl.ds(pl.multiple_of(base + 8 * k, 8), 8), :] = jnp.concatenate(fours, axis=0)
        arrive(send(all_ref.at[turn, pl.ds(pl.multiple_of(base, 32), 32)], zs_sem, zr_sem, along_z))
        base = pl.multiple_of(core * 256, 256)
        copies = send(all_ref.at[turn, pl.ds(base, 256)], cs_sem, cr_sem, other)
        total = coarse_half(turn, core)
        arrive(copies)
        total = jnp.where(part_mask, total + coarse_half(turn, 1 - core), 0.0)
        total = jnp.sum(total.reshape(4, 8, 256), axis=0)
        total = over_groups(total[:, 0:128] + total[:, 128:256])
        coarse = [total[s : s + 1] + total[s + 4 : s + 5] for s in range(SAMPLES)]
        if turn == 0:
            return coarse, None
        sums = all_ref[turn, 0:8, :]
        for k in range(1, 64):
            sums = sums + all_ref[turn, 8 * k : 8 * k + 8, :]
        return coarse, over_groups(sums[3:4] + sums[7:8])

    def scalar_line(rows):
        stacked = jnp.zeros((16, 128), F32)
        for k, value in enumerate(rows):
            stacked = jnp.where(rows16 == k, value, stacked)
        summed = jnp.sum(stacked, axis=1, keepdims=True)
        placed = jnp.where(rows16 == (lax.broadcasted_iota(I32, (16, 128), 1) & 31), summed, 0.0)
        return jnp.sum(placed, axis=0, keepdims=True)

    def over_nodes(value):
        return jnp.sum(value, axis=0, keepdims=True)

    def fit_row(residual, scale, rhs, coarse, s):
        own = over_nodes(weight * residual * residual * scale)
        return own + jnp.where(lane_row < NC, rhs[s] * coarse[s], 0.0)

    samples = range(SAMPLES)

    residual = halo_finish(0, load_halo, load)
    rhs = restrict(residual)
    coarse, _ = everyone(0, rhs, jnp.zeros((1, 128), F32), coarse_setup)
    diag = halo_finish(1, diag_halo, diag)
    inverse_diag = [1.0 / diag[s] for s in samples]
    spread = prolong(coarse)
    copies = halo_start(2, spread)
    spread = halo_finish(2, copies, spread)
    precond = [residual[s] * inverse_diag[s] + spread[s] for s in samples]

    direction = precond
    raw = operate(direction)
    copies = halo_start(3, raw)
    line = scalar_line(
        [fit_row(residual[s], inverse_diag[s], rhs, coarse, s) for s in samples]
        + [over_nodes(direction[s] * raw[s]) for s in samples]
    )
    image = halo_finish(3, copies, raw)
    image_rhs = restrict(image)
    image_coarse, sums = everyone(1, image_rhs, line)
    fit = [sums[:, s : s + 1] for s in samples]
    curved = [sums[:, 3 + s : 4 + s] for s in samples]
    step = [fit[s] / curved[s] for s in samples]
    coarse = [coarse[s] - step[s] * image_coarse[s] for s in samples]
    spread = prolong(coarse)
    copies = halo_start(4, spread)
    solution = [step[s] * direction[s] for s in samples]
    residual = [residual[s] - step[s] * image[s] for s in samples]
    rhs = [rhs[s] - step[s] * image_rhs[s] for s in samples]
    spread = halo_finish(4, copies, spread)
    precond = [residual[s] * inverse_diag[s] + spread[s] for s in samples]

    fresh = operate(precond)
    copies = halo_start(5, fresh)
    line = scalar_line(
        [fit_row(residual[s], inverse_diag[s], rhs, coarse, s) for s in samples]
        + [over_nodes(precond[s] * fresh[s]) for s in samples]
        + [over_nodes(precond[s] * raw[s]) for s in samples]
    )
    fresh_image = halo_finish(5, copies, fresh)
    fresh_rhs = restrict(fresh_image)
    fresh_coarse, sums = everyone(2, fresh_rhs, line)
    fit_next = [sums[:, s : s + 1] for s in samples]
    ratio = [fit_next[s] / fit[s] for s in samples]
    curved = [
        sums[:, 3 + s : 4 + s] + ratio[s] * (2.0 * sums[:, 6 + s : 7 + s] + ratio[s] * curved[s]) for s in samples
    ]
    step = [fit_next[s] / curved[s] for s in samples]
    coarse = [coarse[s] - step[s] * (fresh_coarse[s] + ratio[s] * image_coarse[s]) for s in samples]
    spread = prolong(coarse)
    copies = halo_start(6, spread)
    solution = [solution[s] + step[s] * (precond[s] + ratio[s] * direction[s]) for s in samples]
    residual = [residual[s] - step[s] * (fresh_image[s] + ratio[s] * image[s]) for s in samples]

    def put(ref, values):
        for s in samples:
            for h in range(NH):
                width = min(128, NL - 128 * h)
                ref[s : s + 1, 128 * h : 128 * h + width] = values[s][h : h + 1, 0:width]

    put(sol_ref, solution)
    put(res_ref, residual)
    spread = halo_finish(6, copies, spread)
    put(pre_ref, [residual[s] * inverse_diag[s] + spread[s] for s in samples])
    for copy in pending:
        copy.wait_send()


def body(
    load, node_mass, side_lists, end_lists, connect, geometry, cover, grazing, rates, elem_count, basis, coarse_inverse
):
    vmem = pl.BlockSpec(memory_space=pltpu.VMEM)
    hbm = pl.BlockSpec(memory_space=pltpu.HBM)
    dma = pltpu.SemaphoreType.DMA
    return pl.pallas_call(
        kernel,
        out_shape=[jax.ShapeDtypeStruct((SAMPLES, NL), F32)] * 3,
        in_specs=[hbm] * 12,
        out_specs=[vmem] * 3,
        scratch_shapes=[
            pltpu.VMEM((SAMPLES, NL), F32),
            pltpu.VMEM((NL,), F32),
            pltpu.VMEM((2, SIDE), I32), pltpu.VMEM((2, SIDE), I32),
            pltpu.SMEM((2, SIDE), I32), pltpu.SMEM((2, SIDE), I32),
            pltpu.VMEM((3, EL), I32),
            pltpu.VMEM((4, EL), F32),
            pltpu.VMEM((16, 128), F32),
            pltpu.VMEM((16, 128), F32),
            pltpu.SMEM((SAMPLES,), F32),
            pltpu.SMEM((1,), I32),
            pltpu.VMEM((NC, NL), F32),
            pltpu.VMEM((NC, 512 * NC), BF16),
            pltpu.VMEM((3, 16, 128), I32),
            pltpu.VMEM((3, 16, 128), I32),
            pltpu.VMEM((4, 16, 128), F32),
            pltpu.VMEM((SAMPLES, 16, 128), F32),
            pltpu.VMEM((SAMPLES, 2, 3, 16, 128), F32),
            pltpu.VMEM((96, 3 * EL), BF16),
            pltpu.VMEM((128, 3 * EL), BF16),
            pltpu.VMEM((16, 128), F32),
            pltpu.VMEM((5, 16, 128), I32),
            pltpu.VMEM((8, 128), I32),
            pltpu.VMEM((12 * NC, 128), F32),
            pltpu.VMEM((24 * NC, 128), BF16),
            pltpu.VMEM((2, 256, 1024), BF16),
            pltpu.VMEM((3, 512, 128), F32),
            pltpu.VMEM((3, NX * NY, 4, 128), F32),
            pltpu.VMEM((SAMPLES, 16, 128), F32),
            pltpu.VMEM((HALOS, 8, 128), F32),
            pltpu.VMEM((HALOS, 8, 8, 128), F32),
            dma((14,)),
            dma((HALOS, 8)), dma((HALOS, 8)),
            dma((3, NX * NY - 1)), dma((3, NX * NY - 1)),
            dma((3, NZ - 1)), dma((3, NZ - 1)),
            dma((3, 1)), dma((3, 1)),
        ],
        compiler_params=pltpu.CompilerParams(
            collective_id=0, has_side_effects=True, vmem_limit_bytes=56 * 2**20
        ),
    )(
        load, node_mass, side_lists, end_lists, connect, geometry,
        cover.reshape(16, 128), grazing.reshape(16, 128), rates, elem_count, basis, coarse_inverse,
    )


def solution(mesh):
    both = ("row", "col")
    return jax.shard_map(
        body,
        mesh=mesh,
        in_specs=(
            P(None, both), P(both), P(None, both), P(None, both), P(None, both), P(None, both),
            P(both), P(both), P(), P(both), P(None, both), P(both, None),
        ),
        out_specs=(P(None, both), P(None, both), P(None, both)),
        check_vma=False,
    )
```

```python
import functools

import jax
import jax.numpy as jnp
from jax import lax
from jax.experimental import pallas as pl
from jax.experimental.pallas import tpu as pltpu
from jax.sharding import PartitionSpec as P

MESH = pl.DeviceIdType.MESH
F32, BF16, I32 = jnp.float32, jnp.bfloat16, jnp.int32

NX, NZ, NY = 4, 8, 8
N_ROW, N_COL = 32, 16
SIDE, NL, EL, NC, SAMPLES = 33, 1089, 2048, 32, 3
NH = 9
GAP = 40
EMPTY = 36
AROUND = ((-1, -1), (-1, 1), (1, -1), (1, 1), (-1, 0), (1, 0), (0, -1), (0, 1))
HALOS = 4
BLOCKS = 3 * 4 * NC


def take(row, index):
    return jnp.take_along_axis(
        jnp.broadcast_to(row, index.shape), index, axis=1, mode="promise_in_bounds"
    )


def halves(value):
    high = value.astype(BF16)
    return high, (value - high.astype(F32)).astype(BF16)


def dot_lanes(left, right):
    return lax.dot_general(left, right, (((1,), (1,)), ((), ())), preferred_element_type=F32)


def dot_rows(left, right):
    return lax.dot_general(left, right, (((1,), (0,)), ((), ())), preferred_element_type=F32)


def over_groups(row):
    row = row + pltpu.roll(row, 64, 1)
    return row + pltpu.roll(row, 32, 1)


def kernel(
    load_hbm, mass_hbm, side_hbm, end_hbm, conn_hbm, geom_hbm, cover_hbm, graze_hbm,
    rates_hbm, count_hbm, basis_hbm, inv_hbm,
    out_ref,
    load_ref, mass_ref, side_ref, end_ref, side_sm, end_sm, conn_ref, geom_ref, cover_ref, graze_ref,
    rates_sm, count_sm, basis_ref, inv_ref, low_ref, high_ref, geo_ref, cond_ref, piece_ref, left_ref, hot_ref,
    mass_vm, slot_ref, list_ref, wide_ref, spread_ref, coarse_ref, all_ref, first_ref, node_ref,
    halo_out, halo_in, rim_ref, rims_ref, near_ref, swap_out, swap_in, part_out, part_in,
    local_sem, hs_sem, hr_sem, ps_sem, pr_sem, zs_sem, zr_sem, cs_sem, cr_sem, es_sem, er_sem, ts_sem, tr_sem,
):
    row, col = lax.axis_index("row"), lax.axis_index("col")
    x, z, y, core = row // NZ, lax.rem(row, NZ), col // 2, lax.rem(col, 2)

    loads = []
    for source, target in (
        (side_hbm, side_sm), (end_hbm, end_sm), (side_hbm, side_ref), (end_hbm, end_ref), (load_hbm, load_ref),
        (mass_hbm, mass_ref), (conn_hbm, conn_ref), (geom_hbm, geom_ref), (cover_hbm, cover_ref),
        (graze_hbm, graze_ref), (rates_hbm, rates_sm), (count_hbm, count_sm), (basis_hbm, basis_ref), (inv_hbm, inv_ref),
    ):
        loads.append(pltpu.make_async_copy(source, target, local_sem.at[len(loads)]))
        loads[-1].start()
    basis_copy, inv_copy = loads[12:]

    around = [(lax.rem(row + N_ROW + a, N_ROW), lax.rem(col + N_COL + b, N_COL)) for a, b in AROUND]
    offsets = sorted(
        ((a, b) for a in range(NX) for b in range(NY) if a or b), key=lambda o: -min(o[0], NX - o[0]) - min(o[1], NY - o[1])
    )
    plane = [(lax.rem(x + a, NX) * NZ + z, lax.rem(y + b, NY) * 2 + core) for a, b in offsets]
    along_z = [(x * NZ + lax.rem(z + k, NZ), col) for k in (4, 3, 5, 2, 6, 1, 7)]
    other = (row, y * 2 + 1 - core)
    readers = []
    for a in (-1, 1, 0):
        at_row = lax.rem(row + N_ROW + a, N_ROW)
        place = (1 - a) * 4 + core
        readers.append(((at_row, lax.rem(y + NY - 1, NY) * 2 + 1), place + 2))
        readers.append(((at_row, lax.rem(y + 1, NY) * 2), place))
        if a:
            readers.append(((at_row, y * 2), place + 2))
            readers.append(((at_row, y * 2 + 1), place))
        else:
            readers.append((other, place + 2 * core))
    own_place = 4 + (1 - core) * 2 + core
    beyond = [
        (lax.rem(row + N_ROW + a, N_ROW), lax.rem(col + N_COL + b, N_COL)) for a in (-1, 0, 1) for b in (-2, 2)
    ]
    partners = around + plane + along_z + [other] + beyond
    barrier = pltpu.get_barrier_semaphore()
    for device in partners:
        pl.semaphore_signal(barrier, inc=1, device_id=device, device_id_type=MESH)

    lanes8 = lax.broadcasted_iota(I32, (8, 128), 1)
    rows8 = lax.broadcasted_iota(I32, (8, 128), 0)
    rows16 = lax.broadcasted_iota(I32, (16, 128), 0)
    nodes = rows16 * 128 + lax.broadcasted_iota(I32, (16, 128), 1)
    lane_row = lax.broadcasted_iota(I32, (1, 128), 1)
    pending = []

    for copy in loads[:6]:
        copy.wait()
    low_col, high_col = col > 0, col < N_COL - 1
    low_row, high_row = row > 0, row < N_ROW - 1
    slots = []
    for source, which in ((side_sm, 0), (side_sm, 1), (end_sm, 0), (end_sm, 1)):
        place = jnp.full((16, 128), EMPTY, I32)
        for pos in range(SIDE):
            place = jnp.where(nodes == source[which, pos], pos, place)
        slots.append(place)
    corner_slot = jnp.full((16, 128), EMPTY, I32)
    list_ref[...] = jnp.zeros((8, 128), I32)
    list_ref[0:2, 0:SIDE] = side_ref[...] + 1
    list_ref[2:4, 0:SIDE] = end_ref[...] + 1
    listed = list_ref[...]
    for i in range(2):
        for j in range(2):
            both = (slots[i] != EMPTY) & (slots[2 + j] != EMPTY)
            number = jnp.max(jnp.max(jnp.where(both, nodes, -1), axis=0, keepdims=True), axis=1, keepdims=True)
            listed = jnp.where((rows8 == 4) & (lanes8 == 2 * i + j), number + 1, listed)
            corner_slot = jnp.where(both, 2 * (1 - i) + (1 - j), corner_slot)
    slots.append(corner_slot)
    for k in range(5):
        slot_ref[k] = slots[k]
    slot_ref[5] = jnp.where(slots[1] != EMPTY, slots[1] + GAP, slots[0])
    slot_ref[6] = jnp.where(slots[3] != EMPTY, slots[3] + GAP, slots[2])
    slot_ref[7] = jnp.where(corner_slot != EMPTY, corner_slot + 2 * GAP, EMPTY)
    rim_lists = (
        listed[1:2] + pltpu.roll(listed[0:1], GAP, 1) + pltpu.roll(listed[4:5], 2 * GAP, 1) - 1,
        listed[3:4] + pltpu.roll(listed[2:3], GAP, 1) - 1,
    )
    listed = listed + pltpu.roll(listed, GAP, 1) + pltpu.roll(listed, 2 * GAP, 1) - 1
    sample_of = (lanes8 >= GAP).astype(I32) + (lanes8 >= 2 * GAP).astype(I32)
    edge_key = jnp.where(listed >= 0, sample_of * 16 + (listed >> 7), -1)
    edge_low = jnp.where(listed >= 0, listed & 127, 0)

    def one(flag):
        return jnp.where(flag, 1.0, 0.0).astype(F32)

    def shared(place, there):
        return jnp.where(place != EMPTY, one(there), 0.0)

    copies = (1.0 + shared(slots[0], low_col) + shared(slots[1], high_col)) * (
        1.0 + shared(slots[2], low_row) + shared(slots[3], high_row)
    )
    weight = 1.0 / copies

    def edge_tile(vectors):
        tile = jnp.zeros((8, 128), F32)
        for s in range(SAMPLES):
            for h in range(NH):
                tile = jnp.where(edge_key == s * 16 + h, take(vectors[s][h : h + 1, :], edge_low), tile)
        return tile

    def halo_start(slot, vectors):
        halo_out[slot] = edge_tile(vectors)
        copies = []
        for k, device in enumerate(around):
            copy = pltpu.make_async_remote_copy(
                src_ref=halo_out.at[slot], dst_ref=halo_in.at[slot, k],
                send_sem=hs_sem.at[slot, k], recv_sem=hr_sem.at[slot, k],
                device_id=device, device_id_type=MESH,
            )
            copy.start()
            copies.append(copy)
        pending.extend(copies)
        return copies

    def halo_finish(slot, copies, vectors):
        for copy in copies:
            copy.wait_recv()
        arrived = []
        for k, which, there in ((7, 1, low_col), (6, 0, high_col), (5, 3, low_row), (4, 2, high_row)):
            arrived.append(jnp.where(there, halo_in[slot, k, which : which + 1, :], 0.0))
        corner = jnp.zeros((1, 128), F32)
        in_list = lane_row - jnp.where(lane_row >= 2 * GAP, 2 * GAP, jnp.where(lane_row >= GAP, GAP, 0))
        for i in range(2):
            for j in range(2):
                k = AROUND.index((1 - 2 * j, 1 - 2 * i))
                there = (high_col if i else low_col) & (high_row if j else low_row)
                found = jnp.where(there, halo_in[slot, k, 4:5, :], 0.0)
                corner = jnp.where(in_list == 2 * (1 - i) + (1 - j), found, corner)
        arrived.append(corner)
        result = []
        for s in range(SAMPLES):
            total = vectors[s]
            for k in range(5):
                total = total + take(arrived[k], slot_ref[k] + GAP * s)
            result.append(total)
        return result

    node_ref[...] = jnp.zeros((SAMPLES, 16, 128), F32)
    mass_vm[...] = jnp.ones((16, 128), F32)
    for h in range(NH):
        width = min(128, NL - 128 * h)
        mass_vm[h : h + 1, 0:width] = mass_ref[128 * h : 128 * h + width].reshape(1, width)
        for s in range(SAMPLES):
            node_ref[s, h : h + 1, 0:width] = load_ref[s : s + 1, 128 * h : 128 * h + width]
    load = [node_ref[s] for s in range(SAMPLES)]
    mass = mass_vm[...]
    pl.semaphore_wait(barrier, len(partners))
    load_halo = halo_start(0, load)

    for copy in loads[6:12]:
        copy.wait()
    for p in range(3):
        for j in range(16):
            number = conn_ref[p : p + 1, 128 * j : 128 * j + 128]
            low = number & 127
            low_ref[p, j : j + 1, :] = low
            high_ref[p, j : j + 1, :] = number >> 7
            hot = jnp.where(lax.broadcasted_iota(I32, (128, 128), 0) == low, 1.0, 0.0)
            hot_ref[:, p * EL + 128 * j : p * EL + 128 * j + 128] = hot.astype(BF16)
    for k in range(4):
        for j in range(16):
            geo_ref[k, j : j + 1, :] = geom_ref[k : k + 1, 128 * j : 128 * j + 128]
    live = nodes < count_sm[0]
    for s in range(SAMPLES):
        grown = cover_ref[...] * jnp.exp(-rates_sm[s] * graze_ref[...])
        cond_ref[s] = jnp.where(live, grown, 0.0)

    def gradients():
        g0, g1, g2, g3 = (geo_ref[k] for k in range(4))
        return (g0, g1, -g0 - g1), (g2, g3, -g2 - g3)

    def scatter(terms):
        for s in range(SAMPLES):
            for p in range(3):
                high = terms[s][p].astype(BF16).astype(F32)
                piece_ref[s, 0, p] = high
                piece_ref[s, 1, p] = terms[s][p] - high
        for p in range(3):
            for j in range(16):
                here = high_ref[p, j : j + 1, :] == rows16
                for s in range(SAMPLES):
                    for q in range(2):
                        value = jnp.where(here, piece_ref[s, q, p, j : j + 1, :], 0.0)
                        left_ref[32 * s + 16 * q : 32 * s + 16 * q + 16, p * EL + 128 * j : p * EL + 128 * j + 128] = (
                            value.astype(BF16)
                        )
        summed = dot_lanes(left_ref[...], hot_ref[...])
        return [summed[32 * s : 32 * s + 16] + summed[32 * s + 16 : 32 * s + 32] for s in range(SAMPLES)]

    def operate(vectors):
        b_terms, c_terms = gradients()
        terms = []
        for s in range(SAMPLES):
            corner = []
            for p in range(3):
                low, high = low_ref[p], high_ref[p]
                value = jnp.zeros((16, 128), F32)
                for h in range(NH):
                    value = jnp.where(high == h, take(vectors[s][h : h + 1, :], low), value)
                corner.append(value)
            along_b = b_terms[0] * corner[0] + b_terms[1] * corner[1] + b_terms[2] * corner[2]
            along_c = c_terms[0] * corner[0] + c_terms[1] * corner[1] + c_terms[2] * corner[2]
            along_b, along_c = cond_ref[s] * along_b, cond_ref[s] * along_c
            terms.append([b_terms[p] * along_b + c_terms[p] * along_c for p in range(3)])
        summed = scatter(terms)
        return [mass * vectors[s] + summed[s] for s in range(SAMPLES)]

    b_terms, c_terms = gradients()
    squares = [b_terms[p] * b_terms[p] + c_terms[p] * c_terms[p] for p in range(3)]
    diag = scatter([[cond_ref[s] * squares[p] for p in range(3)] for s in range(SAMPLES)])
    diag = [mass + diag[s] for s in range(SAMPLES)]
    diag_halo = halo_start(1, diag)

    basis_copy.wait()
    wide_ref[...] = jnp.zeros((12 * NC, 128), F32)
    for h in range(NH):
        width = min(128, NL - 128 * h)
        wide_ref[NC * h : NC * h + NC, 0:width] = (
            basis_ref[:, 128 * h : 128 * h + width] * weight[h : h + 1, 0:width]
        )
    wide_high, wide_low = halves(wide_ref[...])
    spread_ref[0 : 12 * NC] = wide_high
    spread_ref[12 * NC : 24 * NC] = wide_low

    own_group = lax.broadcasted_iota(I32, (16, 12 * NC), 0) == lax.broadcasted_iota(I32, (16, 12 * NC), 1) // NC

    def restrict(vectors):
        stacked = jnp.concatenate(vectors, axis=0)
        high, low = halves(stacked)
        both = dot_lanes(jnp.concatenate([high, low], axis=0), spread_ref[...])
        both = both[0:48, 0 : 12 * NC] + both[48:96, 0 : 12 * NC] + both[0:48, 12 * NC : 24 * NC]
        result = []
        for s in range(SAMPLES):
            kept = jnp.where(own_group, both[16 * s : 16 * s + 16], 0.0)
            kept = jnp.sum(kept, axis=0, keepdims=True)
            result.append(over_groups(kept[:, 0:128] + kept[:, 128:256] + kept[:, 256:384]))
        return result

    def prolong(coarse):
        pieces = []
        for s in range(SAMPLES):
            line = coarse[s]
            line = jnp.concatenate([line, line, line], axis=1)
            pieces.append(jnp.where(own_group, jnp.broadcast_to(line, (16, 12 * NC)), 0.0))
        high, low = halves(jnp.concatenate(pieces, axis=0))
        first = dot_rows(jnp.concatenate([high, low], axis=0), spread_ref[0 : 12 * NC])
        total = first[0:48] + first[48:96] + dot_rows(high, spread_ref[12 * NC : 24 * NC])
        return [total[16 * s : 16 * s + 16] for s in range(SAMPLES)]

    def rims_start():
        for t in range(2):
            index = jnp.broadcast_to(rim_lists[t], (NC, 128))
            low = jnp.where(index >= 0, index & 127, 0)
            high = jnp.where(index >= 0, index >> 7, -1)
            value = jnp.zeros((NC, 128), F32)
            for h in range(NH):
                value = jnp.where(high == h, take(wide_ref[NC * h : NC * h + NC, :], low), value)
            rim_ref[t] = value
        copies = []
        for k, (a, b) in enumerate(AROUND):
            copy = pltpu.make_async_remote_copy(
                src_ref=rim_ref.at[1 if b == 0 else 0], dst_ref=rims_ref.at[k], send_sem=es_sem.at[k],
                recv_sem=er_sem.at[k], device_id=around[k], device_id_type=MESH,
            )
            copy.start()
            copies.append(copy)
        pending.extend(copies)
        setups.extend(copies)

    def swap_start():
        inv_copy.wait()
        into = lax.broadcasted_iota(I32, (256, 256), 1)
        from_lane = ((into & 127) >> 5) * 64 + (into >> 7) * 32 + (into & 31)
        move = jnp.where(lax.broadcasted_iota(I32, (256, 256), 0) == from_lane, 1.0, 0.0).astype(BF16)
        first_core = core == 0
        for m in range(64):
            part, t = m // 16 * 2 + m % 2, m // 2 % 8
            moved = dot_rows(inv_ref[:, 256 * m : 256 * m + 256], move)
            zero, one_ = moved[:, 0:128], moved[:, 128:256]
            rows, lanes = slice(NC * part, NC * part + NC), slice(128 * t, 128 * t + 128)
            coarse_ref[rows, lanes] = jnp.where(first_core, zero, one_).astype(BF16)
            swap_out[rows, lanes] = jnp.where(first_core, one_, zero)
        copy = pltpu.make_async_remote_copy(
            src_ref=swap_out, dst_ref=swap_in, send_sem=cs_sem.at[0], recv_sem=cr_sem.at[0],
            device_id=other, device_id_type=MESH,
        )
        copy.start()
        pending.append(copy)
        setups.append(copy)

    def setup_start():
        rims_start()
        swap_start()

    def setup_finish():
        for copy in setups:
            copy.wait_recv()
        coarse_ref[256:512, :] = swap_in[...].astype(BF16)
        lanes32 = lax.broadcasted_iota(I32, (NC, 128), 1)
        for k in range(2):
            near_ref[k] = jnp.zeros((BLOCKS, 256), BF16)
        for k, (a, b) in enumerate(AROUND):
            if a == 0 or b == 0:
                start = 0 if a + b == 1 else GAP
                kept = (lanes32 >= start) & (lanes32 < start + SIDE)
            else:
                i, j = (1 - b) // 2, (1 - a) // 2
                kept = lanes32 == 2 * GAP + 2 * (1 - i) + (1 - j)
            if a:
                kept = kept & (low_row if a == 1 else high_row)
            if b:
                kept = kept & (low_col if b == 1 else high_col)
            high, low = halves(jnp.where(kept, rims_ref[k], 0.0))
            at = 128 * (1 - a) + NC * (1 - b)
            lane = 128 if b == 0 else 0
            near_ref[0, at : at + NC, lane : lane + 128] = high
            near_ref[1, at : at + NC, lane : lane + 128] = low

    setups = []
    part_mask = lax.broadcasted_iota(I32, (32, 512), 0) // 4 == (lax.broadcasted_iota(I32, (32, 512), 1) & 255) // NC
    lanes4 = lax.broadcasted_iota(I32, (4, 128), 1)
    rows4 = lax.broadcasted_iota(I32, (4, 128), 0)

    def by_sample(values):
        return jnp.where(rows4 == 0, values[0], jnp.where(rows4 == 1, values[1], values[2]))

    def everyone(turn, rhs, scalars, between=None, later=None):
        tile = jnp.where(rows4 == 3, scalars, by_sample(rhs))
        mine = lanes4 >> 5 == lax.rem(y, 4)
        first_ref[turn, x * NY + y] = jnp.where(mine, tile, 0.0)

        def send(refs, sends, recvs, devices):
            copies = []
            for k, device in enumerate(devices):
                copy = pltpu.make_async_remote_copy(
                    src_ref=refs, dst_ref=refs, send_sem=sends.at[turn, k], recv_sem=recvs.at[turn, k],
                    device_id=device, device_id_type=MESH,
                )
                copy.start()
                copies.append(copy)
            pending.extend(copies)
            return copies

        def arrive(copies):
            for copy in copies:
                copy.wait_recv()

        copies = send(first_ref.at[turn, x * NY + y], ps_sem, pr_sem, plane)
        if between is not None:
            between()
        arrive(copies)
        base = (core * NZ + z) * 32
        for k in range(NX):
            fours = []
            for q in range(2):
                four = first_ref[turn, k * NY + 4 * q]
                for j in range(1, 4):
                    four = four + first_ref[turn, k * NY + 4 * q + j]
                fours.append(four)
            all_ref[turn, pl.ds(pl.multiple_of(base + 8 * k, 8), 8), :] = jnp.concatenate(fours, axis=0)
        copies = send(all_ref.at[turn, pl.ds(pl.multiple_of(base, 32), 32)], zs_sem, zr_sem, along_z)
        if later is not None:
            later()
        arrive(copies)
        half = pl.multiple_of(core * 256, 256)
        gathered = [all_ref[turn, pl.ds(pl.multiple_of(half + 32 * t, 32), 32), :] for t in range(8)]
        high, low = halves(jnp.concatenate(gathered, axis=1))
        total = dot_lanes(jnp.concatenate([high, low], axis=0), coarse_ref[...])
        total = jnp.where(part_mask, total[0:32] + total[32:64], 0.0)
        total = total[0:8] + total[8:16] + total[16:24] + total[24:32]
        total = total[0:4] + total[4:8]
        mine = over_groups(total[:, 0:128] + total[:, 128:256])
        others = over_groups(total[:, 256:384] + total[:, 384:512])
        tile = jnp.where(lanes4 >> 5 == core, mine, jnp.where(lanes4 >> 5 == 1 - core, others, 0.0))
        if turn:
            sums = gathered[0]
            for piece in gathered[1:]:
                sums = sums + piece
            sums = sums[0:8] + sums[8:16] + sums[16:24] + sums[24:32]
            sums = over_groups(sums[3:4] + sums[7:8])
            tile = jnp.where(rows4 == 3, jnp.where(lanes4 < 32, sums, 0.0), tile)
        else:
            tile = jnp.where(rows4 == 3, 0.0, tile)
        part_out[turn] = tile
        part_in[turn, own_place] = tile
        for k, (device, place) in enumerate(readers):
            copy = pltpu.make_async_remote_copy(
                src_ref=part_out.at[turn], dst_ref=part_in.at[turn, place], send_sem=ts_sem.at[turn, k],
                recv_sem=tr_sem.at[turn, place], device_id=device, device_id_type=MESH,
            )
            copy.start()
            pending.append(copy)

    def everyone_finish(turn):
        for place in (0, 1, 2, 3, 8, 9, 10, 11, 4, 7, 5 + core):
            pltpu.make_async_remote_copy(
                src_ref=part_out.at[turn], dst_ref=part_in.at[turn, place], send_sem=ts_sem.at[turn, 0],
                recv_sem=tr_sem.at[turn, place], device_id=other, device_id_type=MESH,
            ).wait_recv()
        tiles = []
        for k in range(3):
            left = part_in[turn, 4 * k] + part_in[turn, 4 * k + 1]
            right = part_in[turn, 4 * k + 2] + part_in[turn, 4 * k + 3]
            if k == 1:
                sums = jnp.where(core == 0, right, left)[3:4]
            whole = left + pltpu.roll(right, 64, 1)
            tiles.append(jnp.where(core == 0, pltpu.roll(whole, 96, 1), whole))
        return tiles, sums

    def own_coarse(tiles):
        own = over_groups(jnp.where(lanes4 >> 5 == 1, tiles[1], 0.0))
        return [own[s : s + 1] for s in range(SAMPLES)]

    def spread_all(tiles):
        values = prolong(own_coarse(tiles))
        high, low = halves(jnp.concatenate(tiles, axis=1))
        both = dot_rows(jnp.concatenate([high, low], axis=0), near_ref[0])
        both = both[0:4] + both[4:8] + dot_rows(high, near_ref[1])
        for s in range(SAMPLES):
            side, end = both[s : s + 1, 0:128], both[s : s + 1, 128:256]
            values[s] = values[s] + take(side, slot_ref[5]) + take(side, slot_ref[7]) + take(end, slot_ref[6])
        return values

    def scalar_line(rows):
        stacked = jnp.zeros((16, 128), F32)
        for k, value in enumerate(rows):
            stacked = jnp.where(rows16 == k, value, stacked)
        summed = jnp.sum(stacked, axis=1, keepdims=True)
        placed = jnp.where(rows16 == (lax.broadcasted_iota(I32, (16, 128), 1) & 31), summed, 0.0)
        return jnp.sum(placed, axis=0, keepdims=True)

    def over_nodes(value):
        return jnp.sum(value, axis=0, keepdims=True)

    def fit_row(residual, scale, rhs, coarse, s):
        own = over_nodes(weight * residual * residual * scale)
        return own + jnp.where(lane_row < NC, rhs[s] * coarse[s], 0.0)

    samples = range(SAMPLES)

    residual = halo_finish(0, load_halo, load)
    rhs = restrict(residual)
    everyone(0, rhs, jnp.zeros((1, 128), F32), setup_start, setup_finish)
    diag = halo_finish(1, diag_halo, diag)
    inverse_diag = [1.0 / diag[s] for s in samples]
    tiles, _ = everyone_finish(0)
    spread = spread_all(tiles)
    precond = [residual[s] * inverse_diag[s] + spread[s] for s in samples]

    direction = precond
    raw = operate(direction)
    copies = halo_start(2, raw)
    coarse = own_coarse(tiles)
    line = scalar_line(
        [fit_row(residual[s], inverse_diag[s], rhs, coarse, s) for s in samples]
        + [over_nodes(direction[s] * raw[s]) for s in samples]
    )
    image = halo_finish(2, copies, raw)
    image_rhs = restrict(image)
    everyone(1, image_rhs, line)
    image_tiles, sums = everyone_finish(1)
    fit = [sums[:, s : s + 1] for s in samples]
    curved = [sums[:, 3 + s : 4 + s] for s in samples]
    step = [fit[s] / curved[s] for s in samples]
    steps = by_sample(step)
    tiles = [tiles[k] - steps * image_tiles[k] for k in range(3)]
    spread = spread_all(tiles)
    solution = [step[s] * direction[s] for s in samples]
    residual = [residual[s] - step[s] * image[s] for s in samples]
    rhs = [rhs[s] - step[s] * image_rhs[s] for s in samples]
    precond = [residual[s] * inverse_diag[s] + spread[s] for s in samples]

    fresh = operate(precond)
    copies = halo_start(3, fresh)
    coarse = own_coarse(tiles)
    line = scalar_line(
        [fit_row(residual[s], inverse_diag[s], rhs, coarse, s) for s in samples]
        + [over_nodes(precond[s] * fresh[s]) for s in samples]
        + [over_nodes(precond[s] * raw[s]) for s in samples]
    )
    fresh_image = halo_finish(3, copies, fresh)
    fresh_rhs = restrict(fresh_image)
    everyone(2, fresh_rhs, line)
    fresh_tiles, sums = everyone_finish(2)
    fit_next = [sums[:, s : s + 1] for s in samples]
    ratio = [fit_next[s] / fit[s] for s in samples]
    curved = [
        sums[:, 3 + s : 4 + s] + ratio[s] * (2.0 * sums[:, 6 + s : 7 + s] + ratio[s] * curved[s]) for s in samples
    ]
    step = [fit_next[s] / curved[s] for s in samples]
    steps, ratios = by_sample(step), by_sample(ratio)
    tiles = [tiles[k] - steps * (fresh_tiles[k] + ratios * image_tiles[k]) for k in range(3)]
    spread = spread_all(tiles)
    solution = [solution[s] + step[s] * (precond[s] + ratio[s] * direction[s]) for s in samples]
    residual = [residual[s] - step[s] * (fresh_image[s] + ratio[s] * image[s]) for s in samples]

    def put(at, values):
        for s in samples:
            for h in range(NH):
                width = min(128, NL - 128 * h)
                out_ref[3 * at + s : 3 * at + s + 1, 128 * h : 128 * h + width] = values[s][h : h + 1, 0:width]

    put(0, solution)
    put(1, residual)
    put(2, [residual[s] * inverse_diag[s] + spread[s] for s in samples])
    for copy in pending:
        copy.wait_send()


def body(
    load, node_mass, side_lists, end_lists, connect, geometry, cover, grazing, rates, elem_count, basis, coarse_inverse
):
    vmem = pl.BlockSpec(memory_space=pltpu.VMEM)
    hbm = pl.BlockSpec(memory_space=pltpu.HBM)
    dma = pltpu.SemaphoreType.DMA
    whole = pl.pallas_call(
        kernel,
        out_shape=[jax.ShapeDtypeStruct((3 * SAMPLES, NL), F32)],
        in_specs=[hbm] * 12,
        out_specs=[vmem],
        scratch_shapes=[
            pltpu.VMEM((SAMPLES, NL), F32),
            pltpu.VMEM((NL,), F32),
            pltpu.VMEM((2, SIDE), I32), pltpu.VMEM((2, SIDE), I32),
            pltpu.SMEM((2, SIDE), I32), pltpu.SMEM((2, SIDE), I32),
            pltpu.VMEM((3, EL), I32),
            pltpu.VMEM((4, EL), F32),
            pltpu.VMEM((16, 128), F32),
            pltpu.VMEM((16, 128), F32),
            pltpu.SMEM((SAMPLES,), F32),
            pltpu.SMEM((1,), I32),
            pltpu.VMEM((NC, NL), F32),
            pltpu.VMEM((NC, 512 * NC), BF16),
            pltpu.VMEM((3, 16, 128), I32),
            pltpu.VMEM((3, 16, 128), I32),
            pltpu.VMEM((4, 16, 128), F32),
            pltpu.VMEM((SAMPLES, 16, 128), F32),
            pltpu.VMEM((SAMPLES, 2, 3, 16, 128), F32),
            pltpu.VMEM((96, 3 * EL), BF16),
            pltpu.VMEM((128, 3 * EL), BF16),
            pltpu.VMEM((16, 128), F32),
            pltpu.VMEM((8, 16, 128), I32),
            pltpu.VMEM((8, 128), I32),
            pltpu.VMEM((12 * NC, 128), F32),
            pltpu.VMEM((24 * NC, 128), BF16),
            pltpu.VMEM((512, 1024), BF16),
            pltpu.VMEM((3, 512, 128), F32),
            pltpu.VMEM((3, NX * NY, 4, 128), F32),
            pltpu.VMEM((SAMPLES, 16, 128), F32),
            pltpu.VMEM((HALOS, 8, 128), F32),
            pltpu.VMEM((HALOS, 8, 8, 128), F32),
            pltpu.VMEM((2, NC, 128), F32),
            pltpu.VMEM((8, NC, 128), F32),
            pltpu.VMEM((2, BLOCKS, 256), BF16),
            pltpu.VMEM((256, 1024), F32), pltpu.VMEM((256, 1024), F32),
            pltpu.VMEM((3, 4, 128), F32), pltpu.VMEM((3, 12, 4, 128), F32),
            dma((14,)),
            dma((HALOS, 8)), dma((HALOS, 8)),
            dma((3, NX * NY - 1)), dma((3, NX * NY - 1)),
            dma((3, NZ - 1)), dma((3, NZ - 1)),
            dma((1,)), dma((1,)),
            dma((8,)), dma((8,)),
            dma((3, 11)), dma((3, 12)),
        ],
        compiler_params=pltpu.CompilerParams(
            collective_id=0, has_side_effects=True, vmem_limit_bytes=56 * 2**20
        ),
    )(
        load, node_mass, side_lists, end_lists, connect, geometry,
        cover.reshape(16, 128), grazing.reshape(16, 128), rates, elem_count, basis, coarse_inverse,
    )[0]
    return whole[0:3], whole[3:6], whole[6:9]


def solution(mesh):
    both = ("row", "col")
    return jax.shard_map(
        body,
        mesh=mesh,
        in_specs=(
            P(None, both), P(both), P(None, both), P(None, both), P(None, both), P(None, both),
            P(both), P(both), P(), P(both), P(None, both), P(both, None),
        ),
        out_specs=(P(None, both), P(None, both), P(None, both)),
        check_vma=False,
    )
```

```python
import functools

import jax
import jax.numpy as jnp
from jax import lax
from jax.experimental import pallas as pl
from jax.experimental.pallas import tpu as pltpu
from jax.sharding import PartitionSpec as P

MESH = pl.DeviceIdType.MESH
F32, BF16, I32 = jnp.float32, jnp.bfloat16, jnp.int32

NX, NZ, NY = 4, 8, 8
N_ROW, N_COL = 32, 16
SIDE, NL, EL, NC, SAMPLES = 33, 1089, 2048, 32, 3
NH = 9
GAP = 40
EMPTY = 36
AROUND = ((-1, -1), (-1, 1), (1, -1), (1, 1), (-1, 0), (1, 0), (0, -1), (0, 1))
HALOS = 4
BLOCKS = 3 * 4 * NC


def take(row, index):
    return jnp.take_along_axis(
        jnp.broadcast_to(row, index.shape), index, axis=1, mode="promise_in_bounds"
    )


def halves(value):
    high = value.astype(BF16)
    return high, (value - high.astype(F32)).astype(BF16)


def dot_lanes(left, right):
    return lax.dot_general(left, right, (((1,), (1,)), ((), ())), preferred_element_type=F32)


def dot_rows(left, right):
    return lax.dot_general(left, right, (((1,), (0,)), ((), ())), preferred_element_type=F32)


def wait_all(whole, sem, device, sent=False):
    copy = pltpu.make_async_remote_copy(
        src_ref=whole, dst_ref=whole, send_sem=sem, recv_sem=sem, device_id=device, device_id_type=MESH
    )
    (copy.wait_send if sent else copy.wait_recv)()


def over_groups(row):
    row = row + pltpu.roll(row, 64, 1)
    return row + pltpu.roll(row, 32, 1)


def kernel(
    load_hbm, mass_hbm, side_hbm, end_hbm, conn_hbm, geom_hbm, cover_hbm, graze_hbm,
    rates_hbm, count_hbm, basis_hbm, inv_hbm,
    out_ref,
    load_ref, mass_ref, side_ref, end_ref, side_sm, end_sm, conn_ref, geom_ref, cover_ref, graze_ref,
    rates_sm, count_sm, basis_ref, inv_ref, low_ref, high_ref, geo_ref, cond_ref, piece_ref, left_ref, hot_ref,
    mass_vm, slot_ref, list_ref, wide_ref, spread_ref, coarse_ref, all_ref, first_ref, node_ref,
    halo_out, halo_in, rim_ref, rims_ref, near_ref, swap_out, swap_in, part_out, part_in,
    local_sem, hs_sem, hr_sem, ps_sem, pr_sem, zs_sem, zr_sem, cs_sem, cr_sem, es_sem, er_sem, ts_sem, tr_sem,
):
    row, col = lax.axis_index("row"), lax.axis_index("col")
    x, z, y, core = row // NZ, lax.rem(row, NZ), col // 2, lax.rem(col, 2)

    loads = []
    for source, target in (
        (side_hbm, side_sm), (end_hbm, end_sm), (side_hbm, side_ref), (end_hbm, end_ref), (load_hbm, load_ref),
        (mass_hbm, mass_ref), (conn_hbm, conn_ref), (geom_hbm, geom_ref), (cover_hbm, cover_ref),
        (graze_hbm, graze_ref), (rates_hbm, rates_sm), (count_hbm, count_sm), (basis_hbm, basis_ref), (inv_hbm, inv_ref),
    ):
        loads.append(pltpu.make_async_copy(source, target, local_sem.at[len(loads)]))
        loads[-1].start()
    basis_copy, inv_copy = loads[12:]

    around = [(lax.rem(row + N_ROW + a, N_ROW), lax.rem(col + N_COL + b, N_COL)) for a, b in AROUND]
    offsets = sorted(
        ((a, b) for a in range(NX) for b in range(NY) if a or b), key=lambda o: -min(o[0], NX - o[0]) - min(o[1], NY - o[1])
    )
    plane = [(lax.rem(x + a, NX) * NZ + z, lax.rem(y + b, NY) * 2 + core) for a, b in offsets]
    along_z = [(x * NZ + lax.rem(z + k, NZ), col) for k in (4, 3, 5, 2, 6, 1, 7)]
    other = (row, y * 2 + 1 - core)
    readers = []
    for a, b in ((-1, 1), (1, 1), (-1, 0), (1, 0), (0, 1), (0, 0)):
        at_row = lax.rem(row + N_ROW + a, N_ROW)
        place = (1 - a) * 4 + core
        if b:
            readers.append(((at_row, lax.rem(y + NY - 1, NY) * 2 + 1), place + 2))
            readers.append(((at_row, lax.rem(y + 1, NY) * 2), place))
        elif a:
            readers.append(((at_row, y * 2), place + 2))
            readers.append(((at_row, y * 2 + 1), place))
        else:
            readers.append((other, place + 2 * core))
    own_place = 4 + (1 - core) * 2 + core
    beyond = [
        (lax.rem(row + N_ROW + a, N_ROW), lax.rem(col + N_COL + b, N_COL)) for a in (-1, 0, 1) for b in (-2, 2)
    ]
    partners = around + plane + along_z + [other] + beyond
    barrier = pltpu.get_barrier_semaphore()
    for device in partners:
        pl.semaphore_signal(barrier, inc=1, device_id=device, device_id_type=MESH)

    lanes8 = lax.broadcasted_iota(I32, (8, 128), 1)
    rows8 = lax.broadcasted_iota(I32, (8, 128), 0)
    rows16 = lax.broadcasted_iota(I32, (16, 128), 0)
    nodes = rows16 * 128 + lax.broadcasted_iota(I32, (16, 128), 1)
    lane_row = lax.broadcasted_iota(I32, (1, 128), 1)
    pending = []

    for copy in loads[:6]:
        copy.wait()
    low_col, high_col = col > 0, col < N_COL - 1
    low_row, high_row = row > 0, row < N_ROW - 1
    slots = []
    for source, which in ((side_sm, 0), (side_sm, 1), (end_sm, 0), (end_sm, 1)):
        place = jnp.full((16, 128), EMPTY, I32)
        for pos in range(SIDE):
            place = jnp.where(nodes == source[which, pos], pos, place)
        slots.append(place)
    corner_slot = jnp.full((16, 128), EMPTY, I32)
    list_ref[...] = jnp.zeros((8, 128), I32)
    list_ref[0:2, 0:SIDE] = side_ref[...] + 1
    list_ref[2:4, 0:SIDE] = end_ref[...] + 1
    listed = list_ref[...]
    for i in range(2):
        for j in range(2):
            both = (slots[i] != EMPTY) & (slots[2 + j] != EMPTY)
            number = jnp.max(jnp.max(jnp.where(both, nodes, -1), axis=0, keepdims=True), axis=1, keepdims=True)
            listed = jnp.where((rows8 == 4) & (lanes8 == 2 * i + j), number + 1, listed)
            corner_slot = jnp.where(both, 2 * (1 - i) + (1 - j), corner_slot)
    slots.append(corner_slot)
    for k in range(5):
        slot_ref[k] = slots[k]
    slot_ref[5] = jnp.where(slots[1] != EMPTY, slots[1] + GAP, slots[0])
    slot_ref[6] = jnp.where(slots[3] != EMPTY, slots[3] + GAP, slots[2])
    slot_ref[7] = jnp.where(corner_slot != EMPTY, corner_slot + 2 * GAP, EMPTY)
    rim_lists = (
        listed[1:2] + pltpu.roll(listed[0:1], GAP, 1) + pltpu.roll(listed[4:5], 2 * GAP, 1) - 1,
        listed[3:4] + pltpu.roll(listed[2:3], GAP, 1) - 1,
    )
    listed = listed + pltpu.roll(listed, GAP, 1) + pltpu.roll(listed, 2 * GAP, 1) - 1
    sample_of = (lanes8 >= GAP).astype(I32) + (lanes8 >= 2 * GAP).astype(I32)
    edge_key = jnp.where(listed >= 0, sample_of * 16 + (listed >> 7), -1)
    edge_low = jnp.where(listed >= 0, listed & 127, 0)

    def one(flag):
        return jnp.where(flag, 1.0, 0.0).astype(F32)

    def shared(place, there):
        return jnp.where(place != EMPTY, one(there), 0.0)

    copies = (1.0 + shared(slots[0], low_col) + shared(slots[1], high_col)) * (
        1.0 + shared(slots[2], low_row) + shared(slots[3], high_row)
    )
    weight = 1.0 / copies

    def edge_tile(vectors):
        tile = jnp.zeros((8, 128), F32)
        for s in range(SAMPLES):
            for h in range(NH):
                tile = jnp.where(edge_key == s * 16 + h, take(vectors[s][h : h + 1, :], edge_low), tile)
        return tile

    def halo_start(slot, vectors):
        halo_out[slot] = edge_tile(vectors)
        for k, device in enumerate(around):
            pltpu.make_async_remote_copy(
                src_ref=halo_out.at[slot], dst_ref=halo_in.at[slot, k],
                send_sem=hs_sem.at[slot], recv_sem=hr_sem.at[slot],
                device_id=device, device_id_type=MESH,
            ).start()
        pending.append((halo_in.at[slot], hs_sem.at[slot]))

    def halo_finish(slot, vectors):
        wait_all(halo_in.at[slot], hr_sem.at[slot], other)
        arrived = []
        for k, which, there in ((7, 1, low_col), (6, 0, high_col), (5, 3, low_row), (4, 2, high_row)):
            arrived.append(jnp.where(there, halo_in[slot, k, which : which + 1, :], 0.0))
        corner = jnp.zeros((1, 128), F32)
        in_list = lane_row - jnp.where(lane_row >= 2 * GAP, 2 * GAP, jnp.where(lane_row >= GAP, GAP, 0))
        for i in range(2):
            for j in range(2):
                k = AROUND.index((1 - 2 * j, 1 - 2 * i))
                there = (high_col if i else low_col) & (high_row if j else low_row)
                found = jnp.where(there, halo_in[slot, k, 4:5, :], 0.0)
                corner = jnp.where(in_list == 2 * (1 - i) + (1 - j), found, corner)
        arrived.append(corner)
        result = []
        for s in range(SAMPLES):
            total = vectors[s]
            for k in range(5):
                total = total + take(arrived[k], slot_ref[k] + GAP * s)
            result.append(total)
        return result

    node_ref[...] = jnp.zeros((SAMPLES, 16, 128), F32)
    mass_vm[...] = jnp.ones((16, 128), F32)
    for h in range(NH):
        width = min(128, NL - 128 * h)
        mass_vm[h : h + 1, 0:width] = mass_ref[128 * h : 128 * h + width].reshape(1, width)
        for s in range(SAMPLES):
            node_ref[s, h : h + 1, 0:width] = load_ref[s : s + 1, 128 * h : 128 * h + width]
    load = [node_ref[s] for s in range(SAMPLES)]
    mass = mass_vm[...]
    pl.semaphore_wait(barrier, len(partners))
    halo_start(0, load)

    for copy in loads[6:12]:
        copy.wait()
    for p in range(3):
        for j in range(16):
            number = conn_ref[p : p + 1, 128 * j : 128 * j + 128]
            low = number & 127
            low_ref[p, j : j + 1, :] = low
            high_ref[p, j : j + 1, :] = number >> 7
            hot = jnp.where(lax.broadcasted_iota(I32, (128, 128), 0) == low, 1.0, 0.0)
            hot_ref[:, p * EL + 128 * j : p * EL + 128 * j + 128] = hot.astype(BF16)
    for k in range(4):
        for j in range(16):
            geo_ref[k, j : j + 1, :] = geom_ref[k : k + 1, 128 * j : 128 * j + 128]
    live = nodes < count_sm[0]
    for s in range(SAMPLES):
        grown = cover_ref[...] * jnp.exp(-rates_sm[s] * graze_ref[...])
        cond_ref[s] = jnp.where(live, grown, 0.0)

    def gradients():
        g0, g1, g2, g3 = (geo_ref[k] for k in range(4))
        return (g0, g1, -g0 - g1), (g2, g3, -g2 - g3)

    def scatter(terms):
        for s in range(SAMPLES):
            for p in range(3):
                high = terms[s][p].astype(BF16).astype(F32)
                piece_ref[s, 0, p] = high
                piece_ref[s, 1, p] = terms[s][p] - high
        for p in range(3):
            for j in range(16):
                here = high_ref[p, j : j + 1, :] == rows16
                for s in range(SAMPLES):
                    for q in range(2):
                        value = jnp.where(here, piece_ref[s, q, p, j : j + 1, :], 0.0)
                        left_ref[32 * s + 16 * q : 32 * s + 16 * q + 16, p * EL + 128 * j : p * EL + 128 * j + 128] = (
                            value.astype(BF16)
                        )
        summed = dot_lanes(left_ref[...], hot_ref[...])
        return [summed[32 * s : 32 * s + 16] + summed[32 * s + 16 : 32 * s + 32] for s in range(SAMPLES)]

    def operate(vectors):
        b_terms, c_terms = gradients()
        terms = []
        for s in range(SAMPLES):
            corner = []
            for p in range(3):
                low, high = low_ref[p], high_ref[p]
                value = jnp.zeros((16, 128), F32)
                for h in range(NH):
                    value = jnp.where(high == h, take(vectors[s][h : h + 1, :], low), value)
                corner.append(value)
            along_b = b_terms[0] * corner[0] + b_terms[1] * corner[1] + b_terms[2] * corner[2]
            along_c = c_terms[0] * corner[0] + c_terms[1] * corner[1] + c_terms[2] * corner[2]
            along_b, along_c = cond_ref[s] * along_b, cond_ref[s] * along_c
            terms.append([b_terms[p] * along_b + c_terms[p] * along_c for p in range(3)])
        summed = scatter(terms)
        return [mass * vectors[s] + summed[s] for s in range(SAMPLES)]

    b_terms, c_terms = gradients()
    squares = [b_terms[p] * b_terms[p] + c_terms[p] * c_terms[p] for p in range(3)]
    diag = scatter([[cond_ref[s] * squares[p] for p in range(3)] for s in range(SAMPLES)])
    diag = [mass + diag[s] for s in range(SAMPLES)]
    halo_start(1, diag)

    basis_copy.wait()
    wide_ref[...] = jnp.zeros((12 * NC, 128), F32)
    for h in range(NH):
        width = min(128, NL - 128 * h)
        wide_ref[NC * h : NC * h + NC, 0:width] = (
            basis_ref[:, 128 * h : 128 * h + width] * weight[h : h + 1, 0:width]
        )
    wide_high, wide_low = halves(wide_ref[...])
    spread_ref[0 : 12 * NC] = wide_high
    spread_ref[12 * NC : 24 * NC] = wide_low

    own_group = lax.broadcasted_iota(I32, (16, 12 * NC), 0) == lax.broadcasted_iota(I32, (16, 12 * NC), 1) // NC

    def restrict(vectors):
        stacked = jnp.concatenate(vectors, axis=0)
        high, low = halves(stacked)
        both = dot_lanes(jnp.concatenate([high, low], axis=0), spread_ref[...])
        both = both[0:48, 0 : 12 * NC] + both[48:96, 0 : 12 * NC] + both[0:48, 12 * NC : 24 * NC]
        result = []
        for s in range(SAMPLES):
            kept = jnp.where(own_group, both[16 * s : 16 * s + 16], 0.0)
            kept = jnp.sum(kept, axis=0, keepdims=True)
            result.append(over_groups(kept[:, 0:128] + kept[:, 128:256] + kept[:, 256:384]))
        return result

    def prolong(coarse):
        pieces = []
        for s in range(SAMPLES):
            line = coarse[s]
            line = jnp.concatenate([line, line, line], axis=1)
            pieces.append(jnp.where(own_group, jnp.broadcast_to(line, (16, 12 * NC)), 0.0))
        high, low = halves(jnp.concatenate(pieces, axis=0))
        first = dot_rows(jnp.concatenate([high, low], axis=0), spread_ref[0 : 12 * NC])
        total = first[0:48] + first[48:96] + dot_rows(high, spread_ref[12 * NC : 24 * NC])
        return [total[16 * s : 16 * s + 16] for s in range(SAMPLES)]

    def rims_start():
        for t in range(2):
            index = jnp.broadcast_to(rim_lists[t], (NC, 128))
            low = jnp.where(index >= 0, index & 127, 0)
            high = jnp.where(index >= 0, index >> 7, -1)
            value = jnp.zeros((NC, 128), F32)
            for h in range(NH):
                value = jnp.where(high == h, take(wide_ref[NC * h : NC * h + NC, :], low), value)
            rim_ref[t] = value
        for k, (a, b) in enumerate(AROUND):
            pltpu.make_async_remote_copy(
                src_ref=rim_ref.at[1 if b == 0 else 0], dst_ref=rims_ref.at[k], send_sem=es_sem.at[0],
                recv_sem=er_sem.at[0], device_id=around[k], device_id_type=MESH,
            ).start()
        pending.append((rims_ref, es_sem.at[0]))

    def swap_start():
        inv_copy.wait()
        into = lax.broadcasted_iota(I32, (256, 256), 1)
        from_lane = ((into & 127) >> 5) * 64 + (into >> 7) * 32 + (into & 31)
        move = jnp.where(lax.broadcasted_iota(I32, (256, 256), 0) == from_lane, 1.0, 0.0).astype(BF16)
        first_core = core == 0
        for m in range(64):
            part, t = m // 16 * 2 + m % 2, m // 2 % 8
            moved = dot_rows(inv_ref[:, 256 * m : 256 * m + 256], move)
            zero, one_ = moved[:, 0:128], moved[:, 128:256]
            rows, lanes = slice(NC * part, NC * part + NC), slice(128 * t, 128 * t + 128)
            coarse_ref[rows, lanes] = jnp.where(first_core, zero, one_).astype(BF16)
            swap_out[rows, lanes] = jnp.where(first_core, one_, zero)
        pltpu.make_async_remote_copy(
            src_ref=swap_out, dst_ref=swap_in, send_sem=cs_sem.at[0], recv_sem=cr_sem.at[0],
            device_id=other, device_id_type=MESH,
        ).start()
        pending.append((swap_out, cs_sem.at[0]))

    def setup_start():
        rims_start()
        swap_start()

    def setup_finish():
        wait_all(rims_ref, er_sem.at[0], other)
        wait_all(swap_in, cr_sem.at[0], other)
        coarse_ref[256:512, :] = swap_in[...].astype(BF16)
        lanes32 = lax.broadcasted_iota(I32, (NC, 128), 1)
        for k in range(2):
            near_ref[k] = jnp.zeros((BLOCKS, 256), BF16)
        for k, (a, b) in enumerate(AROUND):
            if a == 0 or b == 0:
                start = 0 if a + b == 1 else GAP
                kept = (lanes32 >= start) & (lanes32 < start + SIDE)
            else:
                i, j = (1 - b) // 2, (1 - a) // 2
                kept = lanes32 == 2 * GAP + 2 * (1 - i) + (1 - j)
            if a:
                kept = kept & (low_row if a == 1 else high_row)
            if b:
                kept = kept & (low_col if b == 1 else high_col)
            high, low = halves(jnp.where(kept, rims_ref[k], 0.0))
            at = 128 * (1 - a) + NC * (1 - b)
            lane = 128 if b == 0 else 0
            near_ref[0, at : at + NC, lane : lane + 128] = high
            near_ref[1, at : at + NC, lane : lane + 128] = low

    part_mask = lax.broadcasted_iota(I32, (32, 512), 0) // 4 == (lax.broadcasted_iota(I32, (32, 512), 1) & 255) // NC
    lanes4 = lax.broadcasted_iota(I32, (4, 128), 1)
    rows4 = lax.broadcasted_iota(I32, (4, 128), 0)

    def by_sample(values):
        return jnp.where(rows4 == 0, values[0], jnp.where(rows4 == 1, values[1], values[2]))

    def everyone(turn, rhs, scalars, between=None, later=None):
        tile = jnp.where(rows4 == 3, scalars, by_sample(rhs))
        mine = lanes4 >> 5 == lax.rem(y, 4)
        first_ref[turn, x * NY + y] = jnp.where(mine, tile, 0.0)

        def send(refs, whole, sends, recvs, devices):
            for device in devices:
                pltpu.make_async_remote_copy(
                    src_ref=refs, dst_ref=refs, send_sem=sends.at[turn], recv_sem=recvs.at[turn],
                    device_id=device, device_id_type=MESH,
                ).start()
            pending.append((whole, sends.at[turn]))

        whole = first_ref.at[turn, pl.ds(0, NX * NY - 1)]
        send(first_ref.at[turn, x * NY + y], whole, ps_sem, pr_sem, plane)
        if between is not None:
            between()
        wait_all(whole, pr_sem.at[turn], other)
        base = (core * NZ + z) * 32
        for k in range(NX):
            fours = []
            for q in range(2):
                four = first_ref[turn, k * NY + 4 * q]
                for j in range(1, 4):
                    four = four + first_ref[turn, k * NY + 4 * q + j]
                fours.append(four)
            all_ref[turn, pl.ds(pl.multiple_of(base + 8 * k, 8), 8), :] = jnp.concatenate(fours, axis=0)
        whole = all_ref.at[turn, pl.ds(0, 32 * (NZ - 1))]
        send(all_ref.at[turn, pl.ds(pl.multiple_of(base, 32), 32)], whole, zs_sem, zr_sem, along_z)
        if later is not None:
            later()
        wait_all(whole, zr_sem.at[turn], other)
        half = pl.multiple_of(core * 256, 256)
        gathered = [all_ref[turn, pl.ds(pl.multiple_of(half + 32 * t, 32), 32), :] for t in range(8)]
        high, low = halves(jnp.concatenate(gathered, axis=1))
        total = dot_lanes(jnp.concatenate([high, low], axis=0), coarse_ref[...])
        total = jnp.where(part_mask, total[0:32] + total[32:64], 0.0)
        total = total[0:8] + total[8:16] + total[16:24] + total[24:32]
        total = total[0:4] + total[4:8]
        mine = over_groups(total[:, 0:128] + total[:, 128:256])
        others = over_groups(total[:, 256:384] + total[:, 384:512])
        tile = jnp.where(lanes4 >> 5 == core, mine, jnp.where(lanes4 >> 5 == 1 - core, others, 0.0))
        if turn:
            sums = gathered[0]
            for piece in gathered[1:]:
                sums = sums + piece
            sums = sums[0:8] + sums[8:16] + sums[16:24] + sums[24:32]
            sums = over_groups(sums[3:4] + sums[7:8])
            tile = jnp.where(rows4 == 3, jnp.where(lanes4 < 32, sums, 0.0), tile)
        else:
            tile = jnp.where(rows4 == 3, 0.0, tile)
        part_out[turn] = tile
        part_in[turn, own_place] = tile
        for device, place in readers:
            pltpu.make_async_remote_copy(
                src_ref=part_out.at[turn], dst_ref=part_in.at[turn, place], send_sem=ts_sem.at[turn],
                recv_sem=tr_sem.at[turn], device_id=device, device_id_type=MESH,
            ).start()
        pending.append((part_in.at[turn, pl.ds(0, 11)], ts_sem.at[turn]))

    def everyone_finish(turn):
        wait_all(part_in.at[turn, pl.ds(0, 11)], tr_sem.at[turn], other)
        tiles = []
        for k in range(3):
            left = part_in[turn, 4 * k] + part_in[turn, 4 * k + 1]
            right = part_in[turn, 4 * k + 2] + part_in[turn, 4 * k + 3]
            if k == 1:
                sums = jnp.where(core == 0, right, left)[3:4]
            whole = left + pltpu.roll(right, 64, 1)
            tiles.append(jnp.where(core == 0, pltpu.roll(whole, 96, 1), whole))
        return tiles, sums

    def own_coarse(tiles):
        own = over_groups(jnp.where(lanes4 >> 5 == 1, tiles[1], 0.0))
        return [own[s : s + 1] for s in range(SAMPLES)]

    def spread_all(tiles):
        values = prolong(own_coarse(tiles))
        high, low = halves(jnp.concatenate(tiles, axis=1))
        both = dot_rows(jnp.concatenate([high, low], axis=0), near_ref[0])
        both = both[0:4] + both[4:8] + dot_rows(high, near_ref[1])
        for s in range(SAMPLES):
            side, end = both[s : s + 1, 0:128], both[s : s + 1, 128:256]
            values[s] = values[s] + take(side, slot_ref[5]) + take(side, slot_ref[7]) + take(end, slot_ref[6])
        return values

    def scalar_line(rows):
        stacked = jnp.zeros((16, 128), F32)
        for k, value in enumerate(rows):
            stacked = jnp.where(rows16 == k, value, stacked)
        summed = jnp.sum(stacked, axis=1, keepdims=True)
        placed = jnp.where(rows16 == (lax.broadcasted_iota(I32, (16, 128), 1) & 31), summed, 0.0)
        return jnp.sum(placed, axis=0, keepdims=True)

    def over_nodes(value):
        return jnp.sum(value, axis=0, keepdims=True)

    def fit_row(residual, scale, rhs, coarse, s):
        own = over_nodes(weight * residual * residual * scale)
        return own + jnp.where(lane_row < NC, rhs[s] * coarse[s], 0.0)

    samples = range(SAMPLES)

    residual = halo_finish(0, load)
    rhs = restrict(residual)
    everyone(0, rhs, jnp.zeros((1, 128), F32), setup_start, setup_finish)
    diag = halo_finish(1, diag)
    inverse_diag = [1.0 / diag[s] for s in samples]
    tiles, _ = everyone_finish(0)
    spread = spread_all(tiles)
    precond = [residual[s] * inverse_diag[s] + spread[s] for s in samples]

    direction = precond
    raw = operate(direction)
    halo_start(2, raw)
    coarse = own_coarse(tiles)
    line = scalar_line(
        [fit_row(residual[s], inverse_diag[s], rhs, coarse, s) for s in samples]
        + [over_nodes(direction[s] * raw[s]) for s in samples]
    )
    image = halo_finish(2, raw)
    image_rhs = restrict(image)
    everyone(1, image_rhs, line)
    image_tiles, sums = everyone_finish(1)
    fit = [sums[:, s : s + 1] for s in samples]
    curved = [sums[:, 3 + s : 4 + s] for s in samples]
    step = [fit[s] / curved[s] for s in samples]
    steps = by_sample(step)
    tiles = [tiles[k] - steps * image_tiles[k] for k in range(3)]
    spread = spread_all(tiles)
    solution = [step[s] * direction[s] for s in samples]
    residual = [residual[s] - step[s] * image[s] for s in samples]
    rhs = [rhs[s] - step[s] * image_rhs[s] for s in samples]
    precond = [residual[s] * inverse_diag[s] + spread[s] for s in samples]

    fresh = operate(precond)
    halo_start(3, fresh)
    coarse = own_coarse(tiles)
    line = scalar_line(
        [fit_row(residual[s], inverse_diag[s], rhs, coarse, s) for s in samples]
        + [over_nodes(precond[s] * fresh[s]) for s in samples]
        + [over_nodes(precond[s] * raw[s]) for s in samples]
    )
    fresh_image = halo_finish(3, fresh)
    fresh_rhs = restrict(fresh_image)
    everyone(2, fresh_rhs, line)
    fresh_tiles, sums = everyone_finish(2)
    fit_next = [sums[:, s : s + 1] for s in samples]
    ratio = [fit_next[s] / fit[s] for s in samples]
    curved = [
        sums[:, 3 + s : 4 + s] + ratio[s] * (2.0 * sums[:, 6 + s : 7 + s] + ratio[s] * curved[s]) for s in samples
    ]
    step = [fit_next[s] / curved[s] for s in samples]
    steps, ratios = by_sample(step), by_sample(ratio)
    tiles = [tiles[k] - steps * (fresh_tiles[k] + ratios * image_tiles[k]) for k in range(3)]
    spread = spread_all(tiles)
    solution = [solution[s] + step[s] * (precond[s] + ratio[s] * direction[s]) for s in samples]
    residual = [residual[s] - step[s] * (fresh_image[s] + ratio[s] * image[s]) for s in samples]

    def put(at, values):
        for s in samples:
            for h in range(NH):
                width = min(128, NL - 128 * h)
                out_ref[at, s : s + 1, 128 * h : 128 * h + width] = values[s][h : h + 1, 0:width]

    put(0, solution)
    put(1, residual)
    put(2, [residual[s] * inverse_diag[s] + spread[s] for s in samples])
    for whole, sem in pending:
        wait_all(whole, sem, other, sent=True)


def body(
    load, node_mass, side_lists, end_lists, connect, geometry, cover, grazing, rates, elem_count, basis, coarse_inverse
):
    vmem = pl.BlockSpec(memory_space=pltpu.VMEM)
    hbm = pl.BlockSpec(memory_space=pltpu.HBM)
    dma = pltpu.SemaphoreType.DMA
    whole = pl.pallas_call(
        kernel,
        out_shape=[jax.ShapeDtypeStruct((3, SAMPLES, NL), F32)],
        in_specs=[hbm] * 12,
        out_specs=[vmem],
        scratch_shapes=[
            pltpu.VMEM((SAMPLES, NL), F32),
            pltpu.VMEM((NL,), F32),
            pltpu.VMEM((2, SIDE), I32), pltpu.VMEM((2, SIDE), I32),
            pltpu.SMEM((2, SIDE), I32), pltpu.SMEM((2, SIDE), I32),
            pltpu.VMEM((3, EL), I32),
            pltpu.VMEM((4, EL), F32),
            pltpu.VMEM((16, 128), F32),
            pltpu.VMEM((16, 128), F32),
            pltpu.SMEM((SAMPLES,), F32),
            pltpu.SMEM((1,), I32),
            pltpu.VMEM((NC, NL), F32),
            pltpu.VMEM((NC, 512 * NC), BF16),
            pltpu.VMEM((3, 16, 128), I32),
            pltpu.VMEM((3, 16, 128), I32),
            pltpu.VMEM((4, 16, 128), F32),
            pltpu.VMEM((SAMPLES, 16, 128), F32),
            pltpu.VMEM((SAMPLES, 2, 3, 16, 128), F32),
            pltpu.VMEM((96, 3 * EL), BF16),
            pltpu.VMEM((128, 3 * EL), BF16),
            pltpu.VMEM((16, 128), F32),
            pltpu.VMEM((8, 16, 128), I32),
            pltpu.VMEM((8, 128), I32),
            pltpu.VMEM((12 * NC, 128), F32),
            pltpu.VMEM((24 * NC, 128), BF16),
            pltpu.VMEM((512, 1024), BF16),
            pltpu.VMEM((3, 512, 128), F32),
            pltpu.VMEM((3, NX * NY, 4, 128), F32),
            pltpu.VMEM((SAMPLES, 16, 128), F32),
            pltpu.VMEM((HALOS, 8, 128), F32),
            pltpu.VMEM((HALOS, 8, 8, 128), F32),
            pltpu.VMEM((2, NC, 128), F32),
            pltpu.VMEM((8, NC, 128), F32),
            pltpu.VMEM((2, BLOCKS, 256), BF16),
            pltpu.VMEM((256, 1024), F32), pltpu.VMEM((256, 1024), F32),
            pltpu.VMEM((3, 4, 128), F32), pltpu.VMEM((3, 12, 4, 128), F32),
            dma((14,)),
            dma((HALOS,)), dma((HALOS,)),
            dma((3,)), dma((3,)),
            dma((3,)), dma((3,)),
            dma((1,)), dma((1,)),
            dma((1,)), dma((1,)),
            dma((3,)), dma((3,)),
        ],
        compiler_params=pltpu.CompilerParams(
            collective_id=0, has_side_effects=True, vmem_limit_bytes=56 * 2**20
        ),
    )(
        load, node_mass, side_lists, end_lists, connect, geometry,
        cover.reshape(16, 128), grazing.reshape(16, 128), rates, elem_count, basis, coarse_inverse,
    )[0]
    return whole[0], whole[1], whole[2]


def solution(mesh):
    both = ("row", "col")
    return jax.shard_map(
        body,
        mesh=mesh,
        in_specs=(
            P(None, both), P(both), P(None, both), P(None, both), P(None, both), P(None, both),
            P(both), P(both), P(), P(both), P(None, both), P(both, None),
        ),
        out_specs=(P(None, both), P(None, both), P(None, both)),
        check_vma=False,
    )
```

```python
import functools

import jax
import jax.numpy as jnp
from jax import lax
from jax.experimental import pallas as pl
from jax.experimental.pallas import tpu as pltpu
from jax.sharding import PartitionSpec as P

MESH = pl.DeviceIdType.MESH
F32, BF16, I32 = jnp.float32, jnp.bfloat16, jnp.int32

NX, NZ, NY = 4, 8, 8
N_ROW, N_COL = 32, 16
SIDE, NL, EL, NC, SAMPLES = 33, 1089, 2048, 32, 3
NH = 9
GAP = 40
EMPTY = 36
AROUND = ((-1, -1), (-1, 1), (1, -1), (1, 1), (-1, 0), (1, 0), (0, -1), (0, 1))
HALOS = 4
BLOCKS = 3 * 4 * NC


def take(row, index):
    return jnp.take_along_axis(
        jnp.broadcast_to(row, index.shape), index, axis=1, mode="promise_in_bounds"
    )


def halves(value):
    high = value.astype(BF16)
    return high, (value - high.astype(F32)).astype(BF16)


def dot_lanes(left, right):
    return lax.dot_general(left, right, (((1,), (1,)), ((), ())), preferred_element_type=F32)


def dot_rows(left, right):
    return lax.dot_general(left, right, (((1,), (0,)), ((), ())), preferred_element_type=F32)


def wait_all(whole, sem, device, sent=False):
    copy = pltpu.make_async_remote_copy(
        src_ref=whole, dst_ref=whole, send_sem=sem, recv_sem=sem, device_id=device, device_id_type=MESH
    )
    (copy.wait_send if sent else copy.wait_recv)()


def over_groups(row):
    row = row + pltpu.roll(row, 64, 1)
    return row + pltpu.roll(row, 32, 1)


def kernel(
    load_hbm, mass_hbm, side_hbm, end_hbm, conn_hbm, geom_hbm, cover_hbm, graze_hbm,
    rates_hbm, count_hbm, basis_hbm, inv_hbm,
    out_ref,
    load_ref, mass_ref, side_ref, end_ref, side_sm, end_sm, conn_ref, geom_ref, cover_ref, graze_ref,
    rates_sm, count_sm, basis_ref, inv_ref, low_ref, high_ref, geo_ref, cond_ref, piece_ref, left_ref, hot_ref,
    mass_vm, slot_ref, list_ref, wide_ref, spread_ref, coarse_ref, all_ref, first_ref, node_ref,
    halo_out, halo_in, rim_ref, rims_ref, near_ref, swap_out, swap_in, part_out, part_in,
    local_sem, hs_sem, hr_sem, ps_sem, pr_sem, zs_sem, zr_sem, fs_sem, fr_sem, cs_sem, cr_sem, es_sem, er_sem, ts_sem, tr_sem,
):
    row, col = lax.axis_index("row"), lax.axis_index("col")
    x, z, y, core = row // NZ, lax.rem(row, NZ), col // 2, lax.rem(col, 2)

    loads = []
    for source, target in (
        (side_hbm, side_sm), (end_hbm, end_sm), (side_hbm, side_ref), (end_hbm, end_ref), (load_hbm, load_ref),
        (mass_hbm, mass_ref), (conn_hbm, conn_ref), (geom_hbm, geom_ref), (cover_hbm, cover_ref),
        (graze_hbm, graze_ref), (rates_hbm, rates_sm), (count_hbm, count_sm), (basis_hbm, basis_ref), (inv_hbm, inv_ref),
    ):
        loads.append(pltpu.make_async_copy(source, target, local_sem.at[len(loads)]))
    for copy in loads[:6]:
        copy.start()
    basis_copy, inv_copy = loads[12:]

    around = [(lax.rem(row + N_ROW + a, N_ROW), lax.rem(col + N_COL + b, N_COL)) for a, b in AROUND]
    offsets = sorted(
        ((a, b) for a in range(NX) for b in range(NY) if a or b), key=lambda o: -min(o[0], NX - o[0]) - min(o[1], NY - o[1])
    )
    plane = [(lax.rem(x + a, NX) * NZ + z, lax.rem(y + b, NY) * 2 + core) for a, b in offsets]
    along_z = [(x * NZ + lax.rem(z + k, NZ), col) for k in (4, 3, 5, 2, 6, 1, 7)]
    other = (row, y * 2 + 1 - core)
    readers = []
    for a, b in ((-1, 1), (1, 1), (-1, 0), (1, 0), (0, 1), (0, 0)):
        at_row = lax.rem(row + N_ROW + a, N_ROW)
        place = (1 - a) * 4 + core
        if b:
            readers.append(((at_row, lax.rem(y + NY - 1, NY) * 2 + 1), place + 2))
            readers.append(((at_row, lax.rem(y + 1, NY) * 2), place))
        elif a:
            readers.append(((at_row, y * 2), place + 2))
            readers.append(((at_row, y * 2 + 1), place))
        else:
            readers.append((other, place + 2 * core))
    own_place = 4 + (1 - core) * 2 + core
    beyond = [(lax.rem(row + N_ROW + a, N_ROW), lax.rem(col + N_COL + b, N_COL)) for a in (-1, 1) for b in (-2, 2)]
    partners = around + beyond + plane + along_z
    barrier = pltpu.get_barrier_semaphore()
    for device in partners:
        pl.semaphore_signal(barrier, inc=1, device_id=device, device_id_type=MESH)

    for copy in loads[6:]:
        copy.start()

    lanes8 = lax.broadcasted_iota(I32, (8, 128), 1)
    rows8 = lax.broadcasted_iota(I32, (8, 128), 0)
    rows16 = lax.broadcasted_iota(I32, (16, 128), 0)
    nodes = rows16 * 128 + lax.broadcasted_iota(I32, (16, 128), 1)
    lane_row = lax.broadcasted_iota(I32, (1, 128), 1)
    pending = []

    for copy in loads[:6]:
        copy.wait()
    low_col, high_col = col > 0, col < N_COL - 1
    low_row, high_row = row > 0, row < N_ROW - 1
    slots = []
    for source, which in ((side_sm, 0), (side_sm, 1), (end_sm, 0), (end_sm, 1)):
        place = jnp.full((16, 128), EMPTY, I32)
        for pos in range(SIDE):
            place = jnp.where(nodes == source[which, pos], pos, place)
        slots.append(place)
    corner_slot = jnp.full((16, 128), EMPTY, I32)
    list_ref[...] = jnp.zeros((8, 128), I32)
    list_ref[0:2, 0:SIDE] = side_ref[...] + 1
    list_ref[2:4, 0:SIDE] = end_ref[...] + 1
    listed = list_ref[...]
    for i in range(2):
        for j in range(2):
            both = (slots[i] != EMPTY) & (slots[2 + j] != EMPTY)
            number = jnp.max(jnp.max(jnp.where(both, nodes, -1), axis=0, keepdims=True), axis=1, keepdims=True)
            listed = jnp.where((rows8 == 4) & (lanes8 == 2 * i + j), number + 1, listed)
            corner_slot = jnp.where(both, 2 * (1 - i) + (1 - j), corner_slot)
    slots.append(corner_slot)
    for k in range(5):
        slot_ref[k] = slots[k]
    slot_ref[5] = jnp.where(slots[1] != EMPTY, slots[1] + GAP, slots[0])
    slot_ref[6] = jnp.where(slots[3] != EMPTY, slots[3] + GAP, slots[2])
    slot_ref[7] = jnp.where(corner_slot != EMPTY, corner_slot + 2 * GAP, EMPTY)
    rim_lists = (
        listed[1:2] + pltpu.roll(listed[0:1], GAP, 1) + pltpu.roll(listed[4:5], 2 * GAP, 1) - 1,
        listed[3:4] + pltpu.roll(listed[2:3], GAP, 1) - 1,
    )
    listed = listed + pltpu.roll(listed, GAP, 1) + pltpu.roll(listed, 2 * GAP, 1) - 1
    sample_of = (lanes8 >= GAP).astype(I32) + (lanes8 >= 2 * GAP).astype(I32)
    edge_key = jnp.where(listed >= 0, sample_of * 16 + (listed >> 7), -1)
    edge_low = jnp.where(listed >= 0, listed & 127, 0)

    def one(flag):
        return jnp.where(flag, 1.0, 0.0).astype(F32)

    def shared(place, there):
        return jnp.where(place != EMPTY, one(there), 0.0)

    copies = (1.0 + shared(slots[0], low_col) + shared(slots[1], high_col)) * (
        1.0 + shared(slots[2], low_row) + shared(slots[3], high_row)
    )
    weight = 1.0 / copies

    def edge_tile(vectors):
        tile = jnp.zeros((8, 128), F32)
        for s in range(SAMPLES):
            for h in range(NH):
                tile = jnp.where(edge_key == s * 16 + h, take(vectors[s][h : h + 1, :], edge_low), tile)
        return tile

    def halo_start(slot, vectors):
        halo_out[slot] = edge_tile(vectors)
        for k, device in enumerate(around):
            pltpu.make_async_remote_copy(
                src_ref=halo_out.at[slot], dst_ref=halo_in.at[slot, k],
                send_sem=hs_sem.at[slot], recv_sem=hr_sem.at[slot],
                device_id=device, device_id_type=MESH,
            ).start()
        pending.append((halo_in.at[slot], hs_sem.at[slot]))

    def halo_finish(slot, vectors):
        wait_all(halo_in.at[slot], hr_sem.at[slot], other)
        arrived = []
        for k, which, there in ((7, 1, low_col), (6, 0, high_col), (5, 3, low_row), (4, 2, high_row)):
            arrived.append(jnp.where(there, halo_in[slot, k, which : which + 1, :], 0.0))
        corner = jnp.zeros((1, 128), F32)
        in_list = lane_row - jnp.where(lane_row >= 2 * GAP, 2 * GAP, jnp.where(lane_row >= GAP, GAP, 0))
        for i in range(2):
            for j in range(2):
                k = AROUND.index((1 - 2 * j, 1 - 2 * i))
                there = (high_col if i else low_col) & (high_row if j else low_row)
                found = jnp.where(there, halo_in[slot, k, 4:5, :], 0.0)
                corner = jnp.where(in_list == 2 * (1 - i) + (1 - j), found, corner)
        arrived.append(corner)
        result = []
        for s in range(SAMPLES):
            total = vectors[s]
            for k in range(5):
                total = total + take(arrived[k], slot_ref[k] + GAP * s)
            result.append(total)
        return result

    node_ref[...] = jnp.zeros((SAMPLES, 16, 128), F32)
    mass_vm[...] = jnp.ones((16, 128), F32)
    for h in range(NH):
        width = min(128, NL - 128 * h)
        mass_vm[h : h + 1, 0:width] = mass_ref[128 * h : 128 * h + width].reshape(1, width)
        for s in range(SAMPLES):
            node_ref[s, h : h + 1, 0:width] = load_ref[s : s + 1, 128 * h : 128 * h + width]
    load = [node_ref[s] for s in range(SAMPLES)]
    mass = mass_vm[...]
    pl.semaphore_wait(barrier, len(partners))
    halo_start(0, load)

    for copy in loads[6:12]:
        copy.wait()
    for p in range(3):
        for j in range(16):
            number = conn_ref[p : p + 1, 128 * j : 128 * j + 128]
            low = number & 127
            low_ref[p, j : j + 1, :] = low
            high_ref[p, j : j + 1, :] = number >> 7
        lows = low_ref[p].astype(F32).T
        for j in range(16):
            hot = jnp.where(lax.broadcasted_iota(I32, (128, 128), 1).astype(F32) == lows[:, j : j + 1], 1.0, 0.0)
            hot_ref[p * EL + 128 * j : p * EL + 128 * j + 128, :] = hot.astype(BF16)
    for k in range(4):
        for j in range(16):
            geo_ref[k, j : j + 1, :] = geom_ref[k : k + 1, 128 * j : 128 * j + 128]
    live = nodes < count_sm[0]
    for s in range(SAMPLES):
        grown = cover_ref[...] * jnp.exp(-rates_sm[s] * graze_ref[...])
        cond_ref[s] = jnp.where(live, grown, 0.0)

    def gradients():
        g0, g1, g2, g3 = (geo_ref[k] for k in range(4))
        return (g0, g1, -g0 - g1), (g2, g3, -g2 - g3)

    def scatter(terms):
        for s in range(SAMPLES):
            for p in range(3):
                high = terms[s][p].astype(BF16).astype(F32)
                piece_ref[s, 0, p] = high
                piece_ref[s, 1, p] = terms[s][p] - high
        for p in range(3):
            for j in range(16):
                here = high_ref[p, j : j + 1, :] == rows16
                for s in range(SAMPLES):
                    for q in range(2):
                        value = jnp.where(here, piece_ref[s, q, p, j : j + 1, :], 0.0)
                        left_ref[32 * s + 16 * q : 32 * s + 16 * q + 16, p * EL + 128 * j : p * EL + 128 * j + 128] = (
                            value.astype(BF16)
                        )
        summed = dot_rows(left_ref[...], hot_ref[...])
        return [summed[32 * s : 32 * s + 16] + summed[32 * s + 16 : 32 * s + 32] for s in range(SAMPLES)]

    def operate(vectors):
        b_terms, c_terms = gradients()
        terms = []
        for s in range(SAMPLES):
            corner = []
            for p in range(3):
                low, high = low_ref[p], high_ref[p]
                value = jnp.zeros((16, 128), F32)
                for h in range(NH):
                    value = jnp.where(high == h, take(vectors[s][h : h + 1, :], low), value)
                corner.append(value)
            along_b = b_terms[0] * corner[0] + b_terms[1] * corner[1] + b_terms[2] * corner[2]
            along_c = c_terms[0] * corner[0] + c_terms[1] * corner[1] + c_terms[2] * corner[2]
            along_b, along_c = cond_ref[s] * along_b, cond_ref[s] * along_c
            terms.append([b_terms[p] * along_b + c_terms[p] * along_c for p in range(3)])
        summed = scatter(terms)
        return [mass * vectors[s] + summed[s] for s in range(SAMPLES)]

    b_terms, c_terms = gradients()
    squares = [b_terms[p] * b_terms[p] + c_terms[p] * c_terms[p] for p in range(3)]
    diag = scatter([[cond_ref[s] * squares[p] for p in range(3)] for s in range(SAMPLES)])
    diag = [mass + diag[s] for s in range(SAMPLES)]
    halo_start(1, diag)

    basis_copy.wait()
    wide_ref[...] = jnp.zeros((12 * NC, 128), F32)
    for h in range(NH):
        width = min(128, NL - 128 * h)
        wide_ref[NC * h : NC * h + NC, 0:width] = (
            basis_ref[:, 128 * h : 128 * h + width] * weight[h : h + 1, 0:width]
        )
    wide_high, wide_low = halves(wide_ref[...])
    spread_ref[0 : 12 * NC] = wide_high
    spread_ref[12 * NC : 24 * NC] = wide_low

    own_group = lax.broadcasted_iota(I32, (16, 12 * NC), 0) == lax.broadcasted_iota(I32, (16, 12 * NC), 1) // NC

    def restrict(vectors):
        stacked = jnp.concatenate(vectors, axis=0)
        high, low = halves(stacked)
        both = dot_lanes(jnp.concatenate([high, low], axis=0), spread_ref[...])
        both = both[0:48, 0 : 12 * NC] + both[48:96, 0 : 12 * NC] + both[0:48, 12 * NC : 24 * NC]
        result = []
        for s in range(SAMPLES):
            kept = jnp.where(own_group, both[16 * s : 16 * s + 16], 0.0)
            kept = jnp.sum(kept, axis=0, keepdims=True)
            result.append(over_groups(kept[:, 0:128] + kept[:, 128:256] + kept[:, 256:384]))
        return result

    def prolong(coarse):
        pieces = []
        for s in range(SAMPLES):
            line = coarse[s]
            line = jnp.concatenate([line, line, line], axis=1)
            pieces.append(jnp.where(own_group, jnp.broadcast_to(line, (16, 12 * NC)), 0.0))
        high, low = halves(jnp.concatenate(pieces, axis=0))
        first = dot_rows(jnp.concatenate([high, low], axis=0), spread_ref[0 : 12 * NC])
        total = first[0:48] + first[48:96] + dot_rows(high, spread_ref[12 * NC : 24 * NC])
        return [total[16 * s : 16 * s + 16] for s in range(SAMPLES)]

    def rims_start():
        for t in range(2):
            index = jnp.broadcast_to(rim_lists[t], (NC, 128))
            low = jnp.where(index >= 0, index & 127, 0)
            high = jnp.where(index >= 0, index >> 7, -1)
            value = jnp.zeros((NC, 128), F32)
            for h in range(NH):
                value = jnp.where(high == h, take(wide_ref[NC * h : NC * h + NC, :], low), value)
            rim_ref[t] = value
        for k, (a, b) in enumerate(AROUND):
            pltpu.make_async_remote_copy(
                src_ref=rim_ref.at[1 if b == 0 else 0], dst_ref=rims_ref.at[k], send_sem=es_sem.at[0],
                recv_sem=er_sem.at[0], device_id=around[k], device_id_type=MESH,
            ).start()
        pending.append((rims_ref, es_sem.at[0]))

    def swap_start():
        inv_copy.wait()
        into = lax.broadcasted_iota(I32, (256, 256), 1)
        from_lane = ((into & 127) >> 5) * 64 + (into >> 7) * 32 + (into & 31)
        move = jnp.where(lax.broadcasted_iota(I32, (256, 256), 0) == from_lane, 1.0, 0.0).astype(BF16)
        first_core = core == 0
        for m in range(64):
            part, t = m // 16 * 2 + m % 2, m // 2 % 8
            moved = dot_rows(inv_ref[:, 256 * m : 256 * m + 256], move)
            zero, one_ = moved[:, 0:128], moved[:, 128:256]
            rows = slice(NC * part, NC * part + NC)
            coarse_ref[t, rows, :] = jnp.where(first_core, zero, one_).astype(BF16)
            swap_out[t, rows, :] = jnp.where(first_core, one_, zero)
        pltpu.make_async_remote_copy(
            src_ref=swap_out, dst_ref=swap_in, send_sem=cs_sem.at[0], recv_sem=cr_sem.at[0],
            device_id=other, device_id_type=MESH,
        ).start()
        pending.append((swap_out, cs_sem.at[0]))

    def setup_start():
        rims_start()
        swap_start()

    def setup_finish():
        wait_all(rims_ref, er_sem.at[0], other)
        wait_all(swap_in, cr_sem.at[0], other)
        coarse_ref[:, 256:512, :] = swap_in[...].astype(BF16)
        lanes32 = lax.broadcasted_iota(I32, (NC, 128), 1)
        for k in range(2):
            near_ref[k] = jnp.zeros((BLOCKS, 256), BF16)
        for k, (a, b) in enumerate(AROUND):
            if a == 0 or b == 0:
                start = 0 if a + b == 1 else GAP
                kept = (lanes32 >= start) & (lanes32 < start + SIDE)
            else:
                i, j = (1 - b) // 2, (1 - a) // 2
                kept = lanes32 == 2 * GAP + 2 * (1 - i) + (1 - j)
            if a:
                kept = kept & (low_row if a == 1 else high_row)
            if b:
                kept = kept & (low_col if b == 1 else high_col)
            high, low = halves(jnp.where(kept, rims_ref[k], 0.0))
            at = 128 * (1 - a) + NC * (1 - b)
            lane = 128 if b == 0 else 0
            near_ref[0, at : at + NC, lane : lane + 128] = high
            near_ref[1, at : at + NC, lane : lane + 128] = low

    part_mask = lax.broadcasted_iota(I32, (32, 512), 0) // 4 == (lax.broadcasted_iota(I32, (32, 512), 1) & 255) // NC
    lanes4 = lax.broadcasted_iota(I32, (4, 128), 1)
    rows4 = lax.broadcasted_iota(I32, (4, 128), 0)

    def by_sample(values):
        return jnp.where(rows4 == 0, values[0], jnp.where(rows4 == 1, values[1], values[2]))

    def everyone(turn, rhs, scalars, between=None, later=None):
        tile = jnp.where(rows4 == 3, scalars, by_sample(rhs))
        mine = lanes4 >> 5 == lax.rem(y, 4)
        first_ref[turn, x * NY + y] = jnp.where(mine, tile, 0.0)

        def send(refs, whole, sends, recvs, devices):
            for device in devices:
                pltpu.make_async_remote_copy(
                    src_ref=refs, dst_ref=refs, send_sem=sends.at[turn], recv_sem=recvs.at[turn],
                    device_id=device, device_id_type=MESH,
                ).start()
            pending.append((whole, sends.at[turn]))

        whole = first_ref.at[turn, pl.ds(0, NX * NY - 1)]
        send(first_ref.at[turn, x * NY + y], whole, ps_sem, pr_sem, plane)
        if between is not None:
            between()
        wait_all(whole, pr_sem.at[turn], other)
        base = (core * NZ + z) * 32
        for k in range(NX):
            fours = []
            for q in range(2):
                four = first_ref[turn, k * NY + 4 * q]
                for j in range(1, 4):
                    four = four + first_ref[turn, k * NY + 4 * q + j]
                fours.append(four)
            all_ref[turn, pl.ds(pl.multiple_of(base + 8 * k, 8), 8), :] = jnp.concatenate(fours, axis=0)
        block = all_ref.at[turn, pl.ds(pl.multiple_of(base, 32), 32)]
        far, near = all_ref.at[turn, pl.ds(0, 96)], all_ref.at[turn, pl.ds(0, 128)]
        send(block, far, fs_sem, fr_sem, along_z[:3])
        send(block, near, zs_sem, zr_sem, along_z[3:])
        if later is not None:
            later()
        half = core * 256
        wait_all(near, zr_sem.at[turn], other)
        total, sums = None, None
        for steps in ((0, 2, 6, 1, 7), (4, 3, 5)):
            at = [lax.rem(z + k, NZ) for k in steps]
            if total is not None:
                wait_all(far, fr_sem.at[turn], other)
            gathered = [all_ref[turn, pl.ds(pl.multiple_of(half + 32 * t, 32), 32), :] for t in at]
            high, low = halves(jnp.concatenate(gathered, axis=1))
            inverse = jnp.concatenate([coarse_ref[t] for t in at], axis=1)
            product = dot_lanes(jnp.concatenate([high, low], axis=0), inverse)
            total = product if total is None else total + product
            for piece in gathered:
                sums = piece if sums is None else sums + piece
        total = jnp.where(part_mask, total[0:32] + total[32:64], 0.0)
        total = total[0:8] + total[8:16] + total[16:24] + total[24:32]
        total = total[0:4] + total[4:8]
        mine = over_groups(total[:, 0:128] + total[:, 128:256])
        others = over_groups(total[:, 256:384] + total[:, 384:512])
        tile = jnp.where(lanes4 >> 5 == core, mine, jnp.where(lanes4 >> 5 == 1 - core, others, 0.0))
        if turn:
            sums = sums[0:8] + sums[8:16] + sums[16:24] + sums[24:32]
            sums = over_groups(sums[3:4] + sums[7:8])
            tile = jnp.where(rows4 == 3, jnp.where(lanes4 < 32, sums, 0.0), tile)
        else:
            tile = jnp.where(rows4 == 3, 0.0, tile)
        part_out[turn] = tile
        part_in[turn, own_place] = tile
        for device, place in readers:
            pltpu.make_async_remote_copy(
                src_ref=part_out.at[turn], dst_ref=part_in.at[turn, place], send_sem=ts_sem.at[turn],
                recv_sem=tr_sem.at[turn], device_id=device, device_id_type=MESH,
            ).start()
        pending.append((part_in.at[turn, pl.ds(0, 11)], ts_sem.at[turn]))

    def everyone_finish(turn):
        wait_all(part_in.at[turn, pl.ds(0, 11)], tr_sem.at[turn], other)
        tiles = []
        for k in range(3):
            left = part_in[turn, 4 * k] + part_in[turn, 4 * k + 1]
            right = part_in[turn, 4 * k + 2] + part_in[turn, 4 * k + 3]
            if k == 1:
                sums = jnp.where(core == 0, right, left)[3:4]
            whole = left + pltpu.roll(right, 64, 1)
            tiles.append(jnp.where(core == 0, pltpu.roll(whole, 96, 1), whole))
        return tiles, sums

    def own_coarse(tiles):
        own = over_groups(jnp.where(lanes4 >> 5 == 1, tiles[1], 0.0))
        return [own[s : s + 1] for s in range(SAMPLES)]

    def spread_all(tiles):
        values = prolong(own_coarse(tiles))
        high, low = halves(jnp.concatenate(tiles, axis=1))
        both = dot_rows(jnp.concatenate([high, low], axis=0), near_ref[0])
        both = both[0:4] + both[4:8] + dot_rows(high, near_ref[1])
        for s in range(SAMPLES):
            side, end = both[s : s + 1, 0:128], both[s : s + 1, 128:256]
            values[s] = values[s] + take(side, slot_ref[5]) + take(side, slot_ref[7]) + take(end, slot_ref[6])
        return values

    def scalar_line(rows):
        stacked = jnp.zeros((16, 128), F32)
        for k, value in enumerate(rows):
            stacked = jnp.where(rows16 == k, value, stacked)
        summed = jnp.sum(stacked, axis=1, keepdims=True)
        placed = jnp.where(rows16 == (lax.broadcasted_iota(I32, (16, 128), 1) & 31), summed, 0.0)
        return jnp.sum(placed, axis=0, keepdims=True)

    def over_nodes(value):
        return jnp.sum(value, axis=0, keepdims=True)

    def fit_row(residual, scale, rhs, coarse, s):
        own = over_nodes(weight * residual * residual * scale)
        return own + jnp.where(lane_row < NC, rhs[s] * coarse[s], 0.0)

    samples = range(SAMPLES)

    residual = halo_finish(0, load)
    rhs = restrict(residual)
    everyone(0, rhs, jnp.zeros((1, 128), F32), setup_start, setup_finish)
    diag = halo_finish(1, diag)
    inverse_diag = [1.0 / diag[s] for s in samples]
    tiles, _ = everyone_finish(0)
    spread = spread_all(tiles)
    precond = [residual[s] * inverse_diag[s] + spread[s] for s in samples]

    direction = precond
    raw = operate(direction)
    halo_start(2, raw)
    coarse = own_coarse(tiles)
    line = scalar_line(
        [fit_row(residual[s], inverse_diag[s], rhs, coarse, s) for s in samples]
        + [over_nodes(direction[s] * raw[s]) for s in samples]
    )
    image = halo_finish(2, raw)
    image_rhs = restrict(image)
    everyone(1, image_rhs, line)
    image_tiles, sums = everyone_finish(1)
    fit = [sums[:, s : s + 1] for s in samples]
    curved = [sums[:, 3 + s : 4 + s] for s in samples]
    step = [fit[s] / curved[s] for s in samples]
    steps = by_sample(step)
    tiles = [tiles[k] - steps * image_tiles[k] for k in range(3)]
    spread = spread_all(tiles)
    solution = [step[s] * direction[s] for s in samples]
    residual = [residual[s] - step[s] * image[s] for s in samples]
    rhs = [rhs[s] - step[s] * image_rhs[s] for s in samples]
    precond = [residual[s] * inverse_diag[s] + spread[s] for s in samples]

    fresh = operate(precond)
    halo_start(3, fresh)
    coarse = own_coarse(tiles)
    line = scalar_line(
        [fit_row(residual[s], inverse_diag[s], rhs, coarse, s) for s in samples]
        + [over_nodes(precond[s] * fresh[s]) for s in samples]
        + [over_nodes(precond[s] * raw[s]) for s in samples]
    )
    fresh_image = halo_finish(3, fresh)
    fresh_rhs = restrict(fresh_image)
    everyone(2, fresh_rhs, line)
    fresh_tiles, sums = everyone_finish(2)
    fit_next = [sums[:, s : s + 1] for s in samples]
    ratio = [fit_next[s] / fit[s] for s in samples]
    curved = [
        sums[:, 3 + s : 4 + s] + ratio[s] * (2.0 * sums[:, 6 + s : 7 + s] + ratio[s] * curved[s]) for s in samples
    ]
    step = [fit_next[s] / curved[s] for s in samples]
    steps, ratios = by_sample(step), by_sample(ratio)
    tiles = [tiles[k] - steps * (fresh_tiles[k] + ratios * image_tiles[k]) for k in range(3)]
    spread = spread_all(tiles)
    solution = [solution[s] + step[s] * (precond[s] + ratio[s] * direction[s]) for s in samples]
    residual = [residual[s] - step[s] * (fresh_image[s] + ratio[s] * image[s]) for s in samples]

    def put(at, values):
        for s in samples:
            for h in range(NH):
                width = min(128, NL - 128 * h)
                out_ref[at, s : s + 1, 128 * h : 128 * h + width] = values[s][h : h + 1, 0:width]

    put(0, solution)
    put(1, residual)
    put(2, [residual[s] * inverse_diag[s] + spread[s] for s in samples])
    for whole, sem in pending:
        wait_all(whole, sem, other, sent=True)


def body(
    load, node_mass, side_lists, end_lists, connect, geometry, cover, grazing, rates, elem_count, basis, coarse_inverse
):
    vmem = pl.BlockSpec(memory_space=pltpu.VMEM)
    hbm = pl.BlockSpec(memory_space=pltpu.HBM)
    dma = pltpu.SemaphoreType.DMA
    whole = pl.pallas_call(
        kernel,
        out_shape=[jax.ShapeDtypeStruct((3, SAMPLES, NL), F32)],
        in_specs=[hbm] * 12,
        out_specs=[vmem],
        scratch_shapes=[
            pltpu.VMEM((SAMPLES, NL), F32),
            pltpu.VMEM((NL,), F32),
            pltpu.VMEM((2, SIDE), I32), pltpu.VMEM((2, SIDE), I32),
            pltpu.SMEM((2, SIDE), I32), pltpu.SMEM((2, SIDE), I32),
            pltpu.VMEM((3, EL), I32),
            pltpu.VMEM((4, EL), F32),
            pltpu.VMEM((16, 128), F32),
            pltpu.VMEM((16, 128), F32),
            pltpu.SMEM((SAMPLES,), F32),
            pltpu.SMEM((1,), I32),
            pltpu.VMEM((NC, NL), F32),
            pltpu.VMEM((NC, 512 * NC), BF16),
            pltpu.VMEM((3, 16, 128), I32),
            pltpu.VMEM((3, 16, 128), I32),
            pltpu.VMEM((4, 16, 128), F32),
            pltpu.VMEM((SAMPLES, 16, 128), F32),
            pltpu.VMEM((SAMPLES, 2, 3, 16, 128), F32),
            pltpu.VMEM((96, 3 * EL), BF16),
            pltpu.VMEM((3 * EL, 128), BF16),
            pltpu.VMEM((16, 128), F32),
            pltpu.VMEM((8, 16, 128), I32),
            pltpu.VMEM((8, 128), I32),
            pltpu.VMEM((12 * NC, 128), F32),
            pltpu.VMEM((24 * NC, 128), BF16),
            pltpu.VMEM((NZ, 512, 128), BF16),
            pltpu.VMEM((3, 512, 128), F32),
            pltpu.VMEM((3, NX * NY, 4, 128), F32),
            pltpu.VMEM((SAMPLES, 16, 128), F32),
            pltpu.VMEM((HALOS, 8, 128), F32),
            pltpu.VMEM((HALOS, 8, 8, 128), F32),
            pltpu.VMEM((2, NC, 128), F32),
            pltpu.VMEM((8, NC, 128), F32),
            pltpu.VMEM((2, BLOCKS, 256), BF16),
            pltpu.VMEM((NZ, 256, 128), F32), pltpu.VMEM((NZ, 256, 128), F32),
            pltpu.VMEM((3, 4, 128), F32), pltpu.VMEM((3, 12, 4, 128), F32),
            dma((14,)),
            dma((HALOS,)), dma((HALOS,)),
            dma((3,)), dma((3,)),
            dma((3,)), dma((3,)),
            dma((3,)), dma((3,)),
            dma((1,)), dma((1,)),
            dma((1,)), dma((1,)),
            dma((3,)), dma((3,)),
        ],
        compiler_params=pltpu.CompilerParams(
            collective_id=0, has_side_effects=True, vmem_limit_bytes=56 * 2**20
        ),
    )(
        load, node_mass, side_lists, end_lists, connect, geometry,
        cover.reshape(16, 128), grazing.reshape(16, 128), rates, elem_count, basis, coarse_inverse,
    )[0]
    return whole[0], whole[1], whole[2]


def solution(mesh):
    both = ("row", "col")
    return jax.shard_map(
        body,
        mesh=mesh,
        in_specs=(
            P(None, both), P(both), P(None, both), P(None, both), P(None, both), P(None, both),
            P(both), P(both), P(), P(both), P(None, both), P(both, None),
        ),
        out_specs=(P(None, both), P(None, both), P(None, both)),
        check_vma=False,
    )
```
